32 devices in a mesh: dp: 4 (over y, x), tensor: 8 (over z, core).
Axes of the slice: x: 2, y: 2, z: 4, core: 2. Of those that a mesh axis runs over, the one named last changes fastest.
Arguments:
- tokens: bfloat16 [8192, 2048], P(('dp', 'tensor')), may hold values from -6 to 6
- lengths: int32 [4, 2], replicated, may hold values from 1 to 1365, as said below
- attention_gain: float32 [2048], replicated, may hold values from 0.25 to 1.75
- attention_shift: float32 [2048], replicated, may hold values from -4 to 4
- query_key_value: bfloat16 [2048, 3, 2048], P(None, None, 'tensor'), may hold values from -0.125 to 0.125
- query_value_bias: float32 [2, 2048], P(None, 'tensor'), may hold values from -4 to 4
- output_weight: bfloat16 [2048, 2048], P('tensor'), may hold values from -0.5 to 0.5
- output_bias: float32 [2048], replicated, may hold values from -4 to 4
- feedforward_gain: float32 [2048], replicated, may hold values from 0.25 to 1.75
- feedforward_shift: float32 [2048], replicated, may hold values from -4 to 4
- expand_weight: bfloat16 [2048, 8192], P(None, 'tensor'), may hold values from -0.125 to 0.125
- expand_bias: float32 [8192], P('tensor'), may hold values from -6 to 6
- contract_weight: bfloat16 [8192, 2048], P('tensor'), may hold values from -0.0625 to 0.0625
- contract_bias: float32 [2048], replicated, may hold values from -4 to 4
- cotangent: bfloat16 [8192, 2048], P(('dp', 'tensor')), may hold values from -6 to 6
Outputs:
- layer_output: bfloat16 [8192, 2048], P(('dp', 'tensor'))
- input_gradient: bfloat16 [8192, 2048], P(('dp', 'tensor'))
- attention_gain_gradient: float32 [2048], P('tensor')
- attention_shift_gradient: float32 [2048], P('tensor')
- projection_gradient: float32 [2048, 3, 2048], P(None, None, 'tensor')
- query_value_gradient: float32 [2, 2048], P(None, 'tensor')
- output_gradient: float32 [2048, 2048], P('tensor')
- output_bias_gradient: float32 [2048], P('tensor')
- feedforward_gain_gradient: float32 [2048], P('tensor')
- feedforward_shift_gradient: float32 [2048], P('tensor')
- expand_gradient: float32 [2048, 8192], P(None, 'tensor')
- expand_bias_gradient: float32 [8192], P('tensor')
- contract_gradient: float32 [8192, 2048], P('tensor')
- contract_bias_gradient: float32 [2048], P('tensor')
The draws below stay inside these ranges and needn't reach their ends.
Inputs may be any that keep to these rules, and one draw needn't show every extreme that they name: Each group's 2 lengths are in order long then short and sum to at most 2048; in exactly one group they sum to 2048, and there the first is 1365.
All inputs are finite; a program needn't handle non-finite values.
Results may differ from the reference program's by a relative error of at most 0.015.
Values may be sent and summed in bfloat16 or wider, within the bound.
No kernel may reach another device: no remote copies, remote signals or barrier semaphores. Data moves between devices by JAX's collectives and lax.ppermute only.
A program may use at most 256 MiB of HBM per device.

```python
import jax
import jax.numpy as jnp
from jax import lax

D = 2048
HEADS = 16
HEAD_DIM = 128
FF = 8192
TOK_GROUP = 2048
GROUPS = 4
TOKENS = 8192


def draw_lengths(key, part):
    key = jax.random.fold_in(key, 11)
    long_most = 2 * TOK_GROUP // 3
    short_most = TOK_GROUP // 6
    key_full, key_long, key_short = jax.random.split(key, 3)
    full_group = jax.random.randint(key_full, (), 0, GROUPS)
    long_part = jax.random.randint(key_long, (GROUPS,), short_most, long_most + 1)
    short_part = jax.random.randint(key_short, (GROUPS,), 1, short_most + 1)
    is_full = jnp.arange(GROUPS) == full_group
    long_part = jnp.where(is_full, long_most, long_part)
    short_part = jnp.where(is_full, TOK_GROUP - long_most, short_part)
    return jnp.stack([long_part, short_part], axis=1).astype(jnp.int32)


def shard_levels(key, shape, cuts, low, largest):
    def one(axis_at, shards_of):
        steps = jax.random.uniform(jax.random.fold_in(jax.random.fold_in(key, 6), axis_at), (shards_of,), jnp.float32, low / len(cuts), largest / len(cuts))
        return jnp.repeat(jnp.exp(steps), shape[axis_at] // shards_of).reshape((-1,) + (1,) * (len(shape) - axis_at - 1))

    loudness = one(*cuts[0])
    for cut in cuts[1:]:
        loudness = loudness * one(*cut)
    return loudness


def normal_values(rng, extent, scale, bound, cuts=(), kind=jnp.bfloat16):
    factor_of = shard_levels(rng, extent, cuts, -0.22, 0.18) if cuts else 1.0
    drawn = jax.random.normal(rng, extent, jnp.float32) * scale * factor_of
    return jnp.minimum(jnp.maximum(drawn, -bound), bound).astype(kind)


def setup_inputs(seed: int = 0) -> dict:
    splits = jax.random.split(jax.random.key(seed), 16)
    tokens = normal_values(splits[0], (TOKENS, D), 1.0, 6.0, ((0, 32),))
    lengths = draw_lengths(jax.random.fold_in(splits[15], 71), 0)
    attention_gain = jnp.clip(1.0 + 0.15 * jax.random.normal(splits[2], (D,), jnp.float32), 0.25, 1.75)
    attention_shift = normal_values(splits[3], (D,), 0.3, 4.0, (), jnp.float32)
    query_key_value = normal_values(splits[4], (D, 3, D), D ** -0.5, 0.125, ((2, 8),))
    query_value_bias = normal_values(splits[5], (2, D), 0.3, 4.0, ((1, 8),), jnp.float32)
    output_weight = normal_values(splits[6], (D, D), (D // 16) ** -0.5, 0.5, ((0, 8),))
    output_bias = normal_values(splits[7], (D,), 0.3, 4.0, (), jnp.float32)
    feedforward_gain = jnp.clip(1.0 + 0.15 * jax.random.normal(splits[8], (D,), jnp.float32), 0.25, 1.75)
    feedforward_shift = normal_values(splits[9], (D,), 0.3, 4.0, (), jnp.float32)
    expand_weight = normal_values(splits[10], (D, FF), D ** -0.5, 0.125, ((1, 8),))
    expand_bias = normal_values(splits[11], (FF,), 0.5, 6.0, ((0, 8),), jnp.float32)
    contract_weight = normal_values(splits[12], (FF, D), FF ** -0.5, 0.0625, ((0, 8),))
    contract_bias = normal_values(splits[13], (D,), 0.3, 4.0, (), jnp.float32)
    cotangent = normal_values(splits[14], (TOKENS, D), 1.0, 6.0, ((0, 32),))
    return {"tokens": tokens, "lengths": lengths, "attention_gain": attention_gain, "attention_shift": attention_shift, "query_key_value": query_key_value, "query_value_bias": query_value_bias, "output_weight": output_weight, "output_bias": output_bias, "feedforward_gain": feedforward_gain, "feedforward_shift": feedforward_shift, "expand_weight": expand_weight, "expand_bias": expand_bias, "contract_weight": contract_weight, "contract_bias": contract_bias, "cotangent": cotangent}


EPSILON = 1e-05
HIGHEST_PRECISION = lax.Precision.HIGHEST

@jax.custom_vjp
def low(v):
    return lax.optimization_barrier(v.astype(jnp.bfloat16)).astype(jnp.float32)

@jax.custom_vjp
def low_back(v):
    return v

def low_keep(v):
    return (low(v), None)

def low_pass(kept, grad):
    return (grad,)

def back_keep(v):
    return (v, None)

def back_low(kept, grad):
    return (low(grad),)
low.defvjp(low_keep, low_pass)
low_back.defvjp(back_keep, back_low)

def layer_norm(values, gain_row, shift_row):
    center = values - lax.optimization_barrier(jnp.mean(values, axis=-1, keepdims=True))
    spread = lax.optimization_barrier(jnp.mean(center * center, axis=-1, keepdims=True))
    return center * lax.rsqrt(spread + EPSILON) * gain_row + shift_row

def segments_of(lengths_row):
    bounds = jnp.cumsum(lengths_row)
    row_index = jnp.arange(TOK_GROUP, dtype=jnp.int32)
    segment = lax.optimization_barrier(jnp.sum((row_index[:, None] >= bounds[None, :]).astype(jnp.int32), axis=1))
    live_mask = (row_index < bounds[-1]).astype(jnp.float32)
    return (segment, live_mask)

def block_forward(input_rows, parameters, segment, live_mask):
    attention_gain, attention_shift, query_key_value, query_value_bias, output_weight, output_bias, feedforward_gain, feedforward_shift, expand_weight, expand_bias, contract_weight, contract_bias = parameters
    normed = low(layer_norm(input_rows, attention_gain, attention_shift))
    full_bias = jnp.stack([query_value_bias[0], jnp.zeros_like(query_value_bias[0]), query_value_bias[1]])
    projected = jnp.einsum('td,dcj->tcj', normed, query_key_value, precision=HIGHEST_PRECISION) + full_bias
    projected = low_back(low(projected))
    split_heads = projected.reshape(TOK_GROUP, 3, HEADS, HEAD_DIM)
    query_heads = split_heads[:, 0]
    key_heads = split_heads[:, 1]
    value_heads = split_heads[:, 2]
    scores = jnp.einsum('qhe,khe->hqk', query_heads, key_heads, precision=HIGHEST_PRECISION) * HEAD_DIM ** (-0.5)
    scores = low_back(scores)
    row_index = jnp.arange(TOK_GROUP, dtype=jnp.int32)
    allowed = (segment[:, None] == segment[None, :]) & (row_index[None, :] <= row_index[:, None])
    scores = jnp.where(allowed[None], scores, -1000000000.0)
    highest = lax.optimization_barrier(jnp.max(scores, axis=-1, keepdims=True))
    exponent = jnp.exp(scores - highest)
    attention = low(exponent / lax.optimization_barrier(jnp.sum(exponent, axis=-1, keepdims=True)))
    context = jnp.einsum('hqk,khe->qhe', attention, value_heads, precision=HIGHEST_PRECISION)
    context = low_back(low(context)).reshape(TOK_GROUP, D)
    attended = low_back(jnp.dot(context, output_weight, precision=HIGHEST_PRECISION))
    hidden = input_rows + attended + output_bias
    mixed = low(layer_norm(hidden, feedforward_gain, feedforward_shift))
    pre_act = low_back(jnp.dot(mixed, expand_weight, precision=HIGHEST_PRECISION) + expand_bias)
    activated = low(jax.nn.gelu(pre_act, approximate=True))
    branch = low_back(jnp.dot(activated, contract_weight, precision=HIGHEST_PRECISION))
    return live_mask[:, None] * (hidden + branch + contract_bias)

def reference(tokens, lengths, attention_gain, attention_shift, query_key_value, query_value_bias, output_weight, output_bias, feedforward_gain, feedforward_shift, expand_weight, expand_bias, contract_weight, contract_bias, cotangent):
    parameters = (attention_gain.astype(jnp.float32), attention_shift.astype(jnp.float32), query_key_value.astype(jnp.float32), query_value_bias.astype(jnp.float32), output_weight.astype(jnp.float32), output_bias.astype(jnp.float32), feedforward_gain.astype(jnp.float32), feedforward_shift.astype(jnp.float32), expand_weight.astype(jnp.float32), expand_bias.astype(jnp.float32), contract_weight.astype(jnp.float32), contract_bias.astype(jnp.float32))
    counts = lax.optimization_barrier(jnp.sum(lengths, axis=1))
    shares = counts.astype(jnp.float32) / jnp.sum(counts).astype(jnp.float32)

    def per_group(running, inputs):
        group_tokens, group_cotangent, group_lengths, group_share = inputs
        segment, live_mask = segments_of(group_lengths)

        def forward(input_rows, weights_all):
            return block_forward(input_rows, weights_all, segment, live_mask)
        result, pullback = jax.vjp(forward, group_tokens.astype(jnp.float32), parameters)
        input_gradient, weight_gradients = pullback(group_cotangent.astype(jnp.float32))
        running = jax.tree.map(lambda total_sum, grad_part: total_sum + group_share * grad_part, running, weight_gradients)
        return (running, (result.astype(jnp.bfloat16), input_gradient.astype(jnp.bfloat16)))
    initial = jax.tree.map(jnp.zeros_like, parameters)
    gradients, (outputs, input_gradients) = lax.scan(per_group, initial, (tokens.reshape(GROUPS, TOK_GROUP, D), cotangent.reshape(GROUPS, TOK_GROUP, D), lengths, shares))
    return (outputs.reshape(TOKENS, D), input_gradients.reshape(TOKENS, D), gradients[0], gradients[1], gradients[2], gradients[3], gradients[4], gradients[5], gradients[6], gradients[7], gradients[8], gradients[9], gradients[10], gradients[11])
```

```python
import functools
import math

import jax
import jax.numpy as jnp
from jax import lax
from jax.experimental import pallas as pl
from jax.experimental.pallas import tpu as pltpu
from jax.sharding import PartitionSpec as P

HEAD_DIM = 128
BLOCK = 512
EPSILON = 1e-05
SCALE = HEAD_DIM ** (-0.5)
SCALE_LOG2 = SCALE * math.log2(math.e)
MASKED = -1e30
VMEM_LIMIT = 48 * 1024 * 1024


def dot(a, b, contract):
    return lax.dot_general(a, b, (contract, ((), ())), preferred_element_type=jnp.float32)


def segment_start(position, first, second):
    return jnp.where(position >= second, second, jnp.where(position >= first, first, 0))


def segment_end(position, first, second, rows):
    return jnp.where(position >= second, rows, jnp.where(position >= first, second, first))


def attend_kernel(block, bounds_ref, q_ref, k_ref, v_ref, out_ref, total_ref):
    query_block = pl.program_id(1)
    first, second = bounds_ref[0], bounds_ref[1]
    offset = query_block * block
    q = q_ref[...]
    q_pos = offset + lax.broadcasted_iota(jnp.int32, (1, block), 1)
    start = segment_start(q_pos, first, second)
    k_row = lax.broadcasted_iota(jnp.int32, (block, block), 0)

    def step(key_block, carry):
        highest, row_sum, acc = carry
        rows = pl.ds(pl.multiple_of(key_block * block, block), block)
        scores = dot(k_ref[rows, :], q, ((1,), (1,)))
        base = key_block * block
        allowed = (k_row <= q_pos - base) & (k_row >= start - base)
        scores = jnp.where(allowed, scores * SCALE_LOG2, MASKED)
        new_highest = jnp.maximum(highest, jnp.max(scores, axis=0, keepdims=True))
        weights = jnp.exp2(scores - new_highest)
        decay = jnp.exp2(highest - new_highest)
        row_sum = row_sum * decay + jnp.sum(weights, axis=0, keepdims=True)
        acc = acc * decay + dot(v_ref[rows, :], weights.astype(jnp.bfloat16), ((0,), (0,)))
        return new_highest, row_sum, acc

    low = segment_start(offset, first, second) // block
    highest, row_sum, acc = lax.fori_loop(
        low,
        query_block + 1,
        step,
        (
            jnp.full((1, block), MASKED, jnp.float32),
            jnp.zeros((1, block), jnp.float32),
            jnp.zeros((HEAD_DIM, block), jnp.float32),
        ),
    )
    out_ref[...] = jnp.transpose(acc / row_sum).astype(jnp.bfloat16)
    total_ref[0] = highest + jnp.log2(row_sum)


def attend(bounds, projected, local_heads):
    rows = projected.shape[0]
    block = min(BLOCK, rows)
    return pl.pallas_call(
        functools.partial(attend_kernel, block),
        grid_spec=pltpu.PrefetchScalarGridSpec(
            num_scalar_prefetch=1,
            grid=(local_heads, rows // block),
            in_specs=[
                pl.BlockSpec((block, HEAD_DIM), lambda h, i, _: (i, h)),
                pl.BlockSpec((rows, HEAD_DIM), lambda h, i, _: (0, local_heads + h)),
                pl.BlockSpec((rows, HEAD_DIM), lambda h, i, _: (0, 2 * local_heads + h)),
            ],
            out_specs=[
                pl.BlockSpec((block, HEAD_DIM), lambda h, i, _: (i, h)),
                pl.BlockSpec((1, 1, block), lambda h, i, _: (h, 0, i)),
            ],
        ),
        out_shape=[
            jax.ShapeDtypeStruct((rows, local_heads * HEAD_DIM), jnp.bfloat16),
            jax.ShapeDtypeStruct((local_heads, 1, rows), jnp.float32),
        ],
        compiler_params=pltpu.CompilerParams(vmem_limit_bytes=VMEM_LIMIT),
        cost_estimate=pl.CostEstimate(
            flops=4 * local_heads * rows * rows * HEAD_DIM,
            bytes_accessed=8 * rows * local_heads * HEAD_DIM,
            transcendentals=local_heads * rows * rows,
        ),
    )(bounds, projected, projected, projected)


def attend_back_kernel(
    block,
    local_heads,
    bounds_ref,
    q_ref,
    k_ref,
    v_ref,
    grad_ref,
    context_ref,
    total_ref,
    out_ref,
    query_acc,
    key_acc,
    value_acc,
    inner_ref,
):
    head = pl.program_id(0)
    first, second = bounds_ref[0], bounds_ref[1]
    rows = q_ref.shape[0]
    width = local_heads * HEAD_DIM
    k_row = lax.broadcasted_iota(jnp.int32, (block, block), 0)
    q_col = lax.broadcasted_iota(jnp.int32, (1, block), 1)
    for i in range(rows // block):
        part = pl.ds(i * block, block)
        product = grad_ref[part, :].astype(jnp.float32) * context_ref[part, :].astype(jnp.float32)
        inner_ref[:, part] = jnp.sum(jnp.transpose(product), axis=0, keepdims=True)
    query_acc[...] = jnp.zeros_like(query_acc)

    def key_step(key_block, _):
        base = pl.multiple_of(key_block * block, block)
        key_rows = pl.ds(base, block)
        key_acc[...] = jnp.zeros_like(key_acc)
        value_acc[...] = jnp.zeros_like(value_acc)

        def query_step(query_block, _):
            offset = pl.multiple_of(query_block * block, block)
            query_rows = pl.ds(offset, block)
            k = k_ref[key_rows, :]
            q = q_ref[query_rows, :]
            grad = grad_ref[query_rows, :]
            q_pos = offset + q_col
            start = segment_start(q_pos, first, second)
            scores = dot(k, q, ((1,), (1,)))
            allowed = (k_row <= q_pos - base) & (k_row >= start - base)
            exponent = jnp.where(
                allowed, scores * SCALE_LOG2 - total_ref[0, :, query_rows], MASKED
            )
            weights = jnp.exp2(exponent)
            grad_weights = dot(v_ref[key_rows, :], grad, ((1,), (1,)))
            score_grad = (weights * (grad_weights - inner_ref[:, query_rows])).astype(jnp.bfloat16)
            value_acc[...] += dot(weights.astype(jnp.bfloat16), grad, ((1,), (0,)))
            key_acc[...] += dot(score_grad, q, ((1,), (0,)))
            query_acc[query_rows, :] += dot(score_grad, k, ((0,), (0,)))
            return 0

        last = segment_end(base + block - 1, first, second, rows) - 1
        lax.fori_loop(key_block, last // block + 1, query_step, 0)
        key_columns = pl.ds(pl.multiple_of(width + head * HEAD_DIM, HEAD_DIM), HEAD_DIM)
        value_columns = pl.ds(pl.multiple_of(2 * width + head * HEAD_DIM, HEAD_DIM), HEAD_DIM)
        out_ref[key_rows, key_columns] = (key_acc[...] * SCALE).astype(jnp.bfloat16)
        out_ref[key_rows, value_columns] = value_acc[...].astype(jnp.bfloat16)
        return 0

    lax.fori_loop(0, rows // block, key_step, 0)
    query_columns = pl.ds(pl.multiple_of(head * HEAD_DIM, HEAD_DIM), HEAD_DIM)
    out_ref[:, query_columns] = (query_acc[...] * SCALE).astype(jnp.bfloat16)


def attend_back(bounds, projected, grad_context, context, totals, local_heads):
    rows = projected.shape[0]
    block = min(BLOCK, rows)
    width = local_heads * HEAD_DIM
    column = pl.BlockSpec((rows, HEAD_DIM), lambda h, _: (0, h))
    return pl.pallas_call(
        functools.partial(attend_back_kernel, block, local_heads),
        grid_spec=pltpu.PrefetchScalarGridSpec(
            num_scalar_prefetch=1,
            grid=(local_heads,),
            in_specs=[
                column,
                pl.BlockSpec((rows, HEAD_DIM), lambda h, _: (0, local_heads + h)),
                pl.BlockSpec((rows, HEAD_DIM), lambda h, _: (0, 2 * local_heads + h)),
                column,
                column,
                pl.BlockSpec((1, 1, rows), lambda h, _: (h, 0, 0)),
            ],
            out_specs=pl.BlockSpec((rows, 3 * width), lambda h, _: (0, 0)),
            scratch_shapes=[
                pltpu.VMEM((rows, HEAD_DIM), jnp.float32),
                pltpu.VMEM((block, HEAD_DIM), jnp.float32),
                pltpu.VMEM((block, HEAD_DIM), jnp.float32),
                pltpu.VMEM((1, rows), jnp.float32),
            ],
        ),
        out_shape=jax.ShapeDtypeStruct((rows, 3 * width), jnp.bfloat16),
        compiler_params=pltpu.CompilerParams(vmem_limit_bytes=VMEM_LIMIT),
        cost_estimate=pl.CostEstimate(
            flops=10 * local_heads * rows * rows * HEAD_DIM,
            bytes_accessed=16 * rows * width,
            transcendentals=local_heads * rows * rows,
        ),
    )(bounds, projected, projected, projected, grad_context, context, totals)


def normalize(values):
    center = values - jnp.mean(values, axis=-1, keepdims=True)
    inverse = lax.rsqrt(jnp.mean(center * center, axis=-1, keepdims=True) + EPSILON)
    return center * inverse, inverse


def normalize_back(grad, gain, unit, inverse):
    scaled = grad * gain
    return inverse * (
        scaled
        - jnp.mean(scaled, axis=-1, keepdims=True)
        - unit * jnp.mean(scaled * unit, axis=-1, keepdims=True)
    )


def gelu_tanh(values):
    return jax.nn.gelu(values, approximate=True)


def after(value, *earlier):
    return lax.optimization_barrier((value,) + earlier)[0]


def ring_order(chips):
    return [c for c in range(chips) if c == 0 or c % 2] + [
        c for c in reversed(range(2, chips)) if c % 2 == 0
    ]


def ring_step(value):
    size = lax.axis_size("tensor")
    order = ring_order(size // 2)
    pairs = []
    for place, chip in enumerate(order):
        following = order[(place + 1) % len(order)]
        pairs += [(2 * chip, 2 * following), (2 * chip + 1, 2 * following + 1)]
    return lax.ppermute(value, "tensor", pairs)


def swap_cores(value):
    return lax.ppermute(value, "tensor", [(i, i ^ 1) for i in range(lax.axis_size("tensor"))])


def ring_chip(step):
    chips = lax.axis_size("tensor") // 2
    order = ring_order(chips)
    places = jnp.array([order.index(c) for c in range(chips)], jnp.int32)
    place = places[lax.axis_index("tensor") // 2]
    return jnp.array(order, jnp.int32)[(place + chips - step) % chips]


def ring_gather(block):
    moving = block
    pairs = []
    for step in range(lax.axis_size("tensor") // 2):
        if step:
            moving = ring_step(moving)
        pairs.append((moving, swap_cores(moving)))
    return pairs


def ring_scatter(part):
    arrived = None
    chips = lax.axis_size("tensor") // 2
    for step in list(range(1, chips)) + [0]:
        mine, other = part(step)
        total = mine.astype(jnp.float32) + swap_cores(other).astype(jnp.float32)
        if arrived is not None:
            total = total + arrived.astype(jnp.float32)
        if step:
            arrived = ring_step(total.astype(jnp.bfloat16))
    return total


def in_order(pairs):
    size = lax.axis_size("tensor")
    core = lax.axis_index("tensor") % 2
    block = pairs[0][0]
    full = jnp.zeros((size,) + block.shape, block.dtype)
    for step, (mine, other) in enumerate(pairs):
        chip = ring_chip(step)
        full = lax.dynamic_update_index_in_dim(full, mine, 2 * chip + core, 0)
        full = lax.dynamic_update_index_in_dim(full, other, 2 * chip + 1 - core, 0)
    return full


def dp_sum(value):
    size = lax.axis_size("dp")
    me = lax.axis_index("dp")
    bits = [1 << i for i in range((size - 1).bit_length())]

    def flip(x, bit):
        return lax.ppermute(x, "dp", [(i, i ^ bit) for i in range(size)])

    def one(x, bits):
        for bit in bits:
            half = x.shape[0] // 2
            up = (me & bit) != 0
            keep = lax.dynamic_slice_in_dim(x, jnp.where(up, half, 0), half)
            give = lax.dynamic_slice_in_dim(x, jnp.where(up, 0, half), half)
            got = flip(give, bit)
            x = (keep.astype(jnp.float32) + got.astype(jnp.float32)).astype(x.dtype)
        for bit in reversed(bits):
            up = (me & bit) != 0
            got = flip(x, bit)
            x = jnp.concatenate([jnp.where(up, got, x), jnp.where(up, x, got)], axis=0)
        return x

    half = value.shape[0] // 2
    return jnp.concatenate([one(value[:half], bits), one(value[half:], bits[::-1])], axis=0)


def small_sum(value, axes):
    for axis in axes:
        size = lax.axis_size(axis)
        bit = 1
        while bit < size:
            value = value + lax.ppermute(value, axis, [(i, i ^ bit) for i in range(size)])
            bit *= 2
    return value


def shards(
    tokens,
    lengths,
    attention_gain,
    attention_shift,
    query_key_value,
    query_value_bias,
    output_weight,
    output_bias,
    feedforward_gain,
    feedforward_shift,
    expand_weight,
    expand_bias,
    contract_weight,
    contract_bias,
    cotangent,
):
    bf16, f32 = jnp.bfloat16, jnp.float32
    shard_rows, features = tokens.shape
    tensor_size = lax.axis_size("tensor")
    group_count = lax.axis_size("dp")
    group = lax.axis_index("dp")
    rank = lax.axis_index("tensor")
    core = rank % 2
    chips = tensor_size // 2
    group_rows = shard_rows * tensor_size
    local_width = query_key_value.shape[2]
    local_heads = local_width // HEAD_DIM
    bounds = jnp.cumsum(lengths, axis=1)
    own_bounds = lax.dynamic_index_in_dim(bounds, group, 0, keepdims=False)
    own_count = own_bounds[-1]
    share = own_count.astype(f32) / jnp.sum(bounds[:, -1]).astype(f32)
    local_rows = rank * shard_rows + jnp.arange(shard_rows, dtype=jnp.int32)
    local_live = (local_rows < own_count).astype(f32)[:, None]

    input_rows = tokens.astype(f32)
    unit_one, inverse_one = normalize(input_rows)
    normed_rows = (unit_one * attention_gain + attention_shift).astype(bf16)
    normed = lax.all_gather(normed_rows, "tensor", axis=0, tiled=True)

    piece = output_weight.shape[0] // group_count
    own_piece = lax.dynamic_slice_in_dim(output_weight, group * piece, piece)
    pieces = in_order(ring_gather(own_piece))
    output_full = lax.all_gather(pieces, "dp", axis=1, tiled=False).reshape(features, features)

    weight_flat = query_key_value.reshape(features, 3 * local_width)
    bias_flat = jnp.concatenate(
        [query_value_bias[0], jnp.zeros_like(query_value_bias[0]), query_value_bias[1]]
    )
    projected = (jnp.dot(normed, weight_flat, preferred_element_type=f32) + bias_flat).astype(bf16)

    grad_rows_low = jnp.where(local_live > 0, cotangent, jnp.zeros_like(cotangent))
    grad_out = [
        jnp.concatenate(pair, axis=0) for pair in ring_gather(after(grad_rows_low, normed))
    ]
    grad_activated = [
        jnp.einsum("td,fd->tf", block, contract_weight, preferred_element_type=f32)
        for block in grad_out
    ]

    context, totals = attend(own_bounds, projected, local_heads)
    context_rows = lax.all_to_all(context, "tensor", split_axis=0, concat_axis=1, tiled=True)
    hidden = (
        input_rows + jnp.dot(context_rows, output_full, preferred_element_type=f32) + output_bias
    )
    unit_two, inverse_two = normalize(hidden)
    mixed_rows = (unit_two * feedforward_gain + feedforward_shift).astype(bf16)

    mixed = [jnp.concatenate(pair, axis=0) for pair in ring_gather(mixed_rows)]
    activated, grad_pre = [None] * chips, [None] * chips
    for step in range(chips):
        pre_act = jnp.dot(mixed[step], expand_weight, preferred_element_type=f32) + expand_bias
        value, gelu_pull = jax.vjp(gelu_tanh, pre_act)
        activated[step] = value.astype(bf16)
        grad_pre[step] = gelu_pull(grad_activated[step])[0].astype(bf16)

    def mixed_part(step):
        part = jnp.einsum(
            "tf,df->td", grad_pre[step], expand_weight, preferred_element_type=f32
        ).astype(bf16)
        return part[:shard_rows], part[shard_rows:]

    grad_mixed = ring_scatter(mixed_part)

    grad_local = grad_rows_low.astype(f32)
    grad_hidden = grad_local + normalize_back(grad_mixed, feedforward_gain, unit_two, inverse_two)
    grad_hidden_low = grad_hidden.astype(bf16)
    grad_context_rows = jnp.einsum(
        "td,jd->tj", grad_hidden_low, output_full, preferred_element_type=f32
    ).astype(bf16)
    grad_context = lax.all_to_all(
        grad_context_rows, "tensor", split_axis=1, concat_axis=0, tiled=True
    )
    projected_grad = attend_back(own_bounds, projected, grad_context, context, totals, local_heads)

    def normed_part(step):
        rows = lax.dynamic_slice_in_dim(
            projected_grad, ring_chip(step) * 2 * shard_rows, 2 * shard_rows
        )
        part = jnp.einsum("tj,dj->td", rows, weight_flat, preferred_element_type=f32).astype(bf16)
        return (
            lax.dynamic_slice_in_dim(part, core * shard_rows, shard_rows),
            lax.dynamic_slice_in_dim(part, (1 - core) * shard_rows, shard_rows),
        )

    grad_normed = ring_scatter(normed_part)
    input_gradient = (
        grad_hidden + normalize_back(grad_normed, attention_gain, unit_one, inverse_one)
    ).astype(bf16)

    def branch_part(step):
        part = jnp.dot(
            after(activated[step], grad_mixed), contract_weight, preferred_element_type=f32
        ).astype(bf16)
        return part[:shard_rows], part[shard_rows:]

    branch = ring_scatter(branch_part)
    layer_output = (local_live * (hidden + branch + contract_bias)).astype(bf16)

    activated_all = jnp.concatenate(activated, axis=0)
    grad_out_all = jnp.concatenate(grad_out, axis=0)
    contract_gradient = dp_sum(
        (
            share
            * jnp.einsum("tf,td->fd", activated_all, grad_out_all, preferred_element_type=f32)
        ).astype(bf16)
    )
    mixed_all = jnp.concatenate(mixed, axis=0)
    grad_pre_all = jnp.concatenate(grad_pre, axis=0)
    expand_gradient = dp_sum(
        (
            share * jnp.einsum("td,tf->df", mixed_all, grad_pre_all, preferred_element_type=f32)
        ).astype(bf16)
    )
    grad_hidden_all = lax.all_gather(
        after(grad_hidden_low, grad_context), "tensor", axis=0, tiled=True
    )
    output_gradient = dp_sum(
        (
            share * jnp.einsum("tj,td->jd", context, grad_hidden_all, preferred_element_type=f32)
        ).astype(bf16)
    )
    projection_gradient = dp_sum(
        (
            share * jnp.einsum("td,tj->dj", normed, projected_grad, preferred_element_type=f32)
        ).astype(bf16)
    ).reshape(features, 3, local_width)

    column_sums = jnp.sum(projected_grad.astype(f32), axis=0)
    sums_by_width = share * jnp.concatenate(
        [
            column_sums[:local_width],
            column_sums[2 * local_width :],
            jnp.sum(grad_pre_all.astype(f32), axis=0),
        ]
    )
    sums_by_width = small_sum(sums_by_width, ("dp",))
    query_value_gradient = sums_by_width[: 2 * local_width].reshape(2, local_width)
    expand_bias_gradient = sums_by_width[2 * local_width :]

    early_sums = share * jnp.stack(
        [
            jnp.sum(grad_hidden, axis=0),
            jnp.sum(grad_mixed * unit_two, axis=0),
            jnp.sum(grad_mixed, axis=0),
            jnp.sum(grad_local, axis=0),
        ]
    )
    late_sums = share * jnp.stack(
        [jnp.sum(grad_normed * unit_one, axis=0), jnp.sum(grad_normed, axis=0)]
    )
    columns = features // tensor_size
    early_sums = lax.dynamic_slice_in_dim(
        small_sum(early_sums, ("tensor", "dp")), rank * columns, columns, 1
    )
    late_sums = lax.dynamic_slice_in_dim(
        small_sum(late_sums, ("tensor", "dp")), rank * columns, columns, 1
    )
    return (
        layer_output,
        input_gradient,
        late_sums[0],
        late_sums[1],
        projection_gradient.astype(f32),
        query_value_gradient,
        output_gradient.astype(f32),
        early_sums[0],
        early_sums[1],
        early_sums[2],
        expand_gradient.astype(f32),
        expand_bias_gradient,
        contract_gradient.astype(f32),
        early_sums[3],
    )


def solution(mesh):
    placed = (
        P(("dp", "tensor"), None),
        P(),
        P(),
        P(),
        P(None, None, "tensor"),
        P(None, "tensor"),
        P("tensor", None),
        P(),
        P(),
        P(),
        P(None, "tensor"),
        P("tensor"),
        P("tensor", None),
        P(),
        P(("dp", "tensor"), None),
    )
    return jax.shard_map(
        shards,
        mesh=mesh,
        in_specs=placed,
        out_specs=(
            P(("dp", "tensor"), None),
            P(("dp", "tensor"), None),
            P("tensor"),
            P("tensor"),
            P(None, None, "tensor"),
            P(None, "tensor"),
            P("tensor", None),
            P("tensor"),
            P("tensor"),
            P("tensor"),
            P(None, "tensor"),
            P("tensor"),
            P("tensor", None),
            P("tensor"),
        ),
        check_vma=False,
    )
```

```python
import functools
import math

import jax
import jax.numpy as jnp
from jax import lax
from jax.experimental import pallas as pl
from jax.experimental.pallas import tpu as pltpu
from jax.sharding import PartitionSpec as P

HEAD_DIM = 128
BLOCK = 512
EPSILON = 1e-05
SCALE = HEAD_DIM ** (-0.5)
SCALE_LOG2 = SCALE * math.log2(math.e)
MASKED = -1e30
VMEM_LIMIT = 48 * 1024 * 1024


def dot(a, b, contract):
    return lax.dot_general(a, b, (contract, ((), ())), preferred_element_type=jnp.float32)


def segment_start(position, first, second):
    return jnp.where(position >= second, second, jnp.where(position >= first, first, 0))


def segment_end(position, first, second, rows):
    return jnp.where(position >= second, rows, jnp.where(position >= first, second, first))


def attend_kernel(block, bounds_ref, q_ref, k_ref, v_ref, out_ref, total_ref):
    query_block = pl.program_id(1)
    first, second = bounds_ref[0], bounds_ref[1]
    offset = query_block * block
    q = q_ref[...]
    q_pos = offset + lax.broadcasted_iota(jnp.int32, (1, block), 1)
    start = segment_start(q_pos, first, second)
    k_row = lax.broadcasted_iota(jnp.int32, (block, block), 0)

    def step(key_block, carry):
        highest, row_sum, acc = carry
        rows = pl.ds(pl.multiple_of(key_block * block, block), block)
        scores = dot(k_ref[rows, :], q, ((1,), (1,)))
        base = key_block * block
        allowed = (k_row <= q_pos - base) & (k_row >= start - base)
        scores = jnp.where(allowed, scores * SCALE_LOG2, MASKED)
        new_highest = jnp.maximum(highest, jnp.max(scores, axis=0, keepdims=True))
        weights = jnp.exp2(scores - new_highest)
        decay = jnp.exp2(highest - new_highest)
        row_sum = row_sum * decay + jnp.sum(weights, axis=0, keepdims=True)
        acc = acc * decay + dot(v_ref[rows, :], weights.astype(jnp.bfloat16), ((0,), (0,)))
        return new_highest, row_sum, acc

    low = segment_start(offset, first, second) // block
    highest, row_sum, acc = lax.fori_loop(
        low,
        query_block + 1,
        step,
        (
            jnp.full((1, block), MASKED, jnp.float32),
            jnp.zeros((1, block), jnp.float32),
            jnp.zeros((HEAD_DIM, block), jnp.float32),
        ),
    )
    out_ref[...] = jnp.transpose(acc / row_sum).astype(jnp.bfloat16)
    total_ref[0] = highest + jnp.log2(row_sum)


def attend(bounds, projected, local_heads):
    rows = projected.shape[0]
    block = min(BLOCK, rows)
    return pl.pallas_call(
        functools.partial(attend_kernel, block),
        grid_spec=pltpu.PrefetchScalarGridSpec(
            num_scalar_prefetch=1,
            grid=(local_heads, rows // block),
            in_specs=[
                pl.BlockSpec((block, HEAD_DIM), lambda h, i, _: (i, h)),
                pl.BlockSpec((rows, HEAD_DIM), lambda h, i, _: (0, local_heads + h)),
                pl.BlockSpec((rows, HEAD_DIM), lambda h, i, _: (0, 2 * local_heads + h)),
            ],
            out_specs=[
                pl.BlockSpec((block, HEAD_DIM), lambda h, i, _: (i, h)),
                pl.BlockSpec((1, 1, block), lambda h, i, _: (h, 0, i)),
            ],
        ),
        out_shape=[
            jax.ShapeDtypeStruct((rows, local_heads * HEAD_DIM), jnp.bfloat16),
            jax.ShapeDtypeStruct((local_heads, 1, rows), jnp.float32),
        ],
        compiler_params=pltpu.CompilerParams(vmem_limit_bytes=VMEM_LIMIT),
        cost_estimate=pl.CostEstimate(
            flops=4 * local_heads * rows * rows * HEAD_DIM,
            bytes_accessed=8 * rows * local_heads * HEAD_DIM,
            transcendentals=local_heads * rows * rows,
        ),
    )(bounds, projected, projected, projected)


def attend_back_kernel(
    block,
    local_heads,
    bounds_ref,
    q_ref,
    k_ref,
    v_ref,
    grad_ref,
    context_ref,
    total_ref,
    out_ref,
    query_acc,
    key_acc,
    value_acc,
    inner_ref,
):
    head = pl.program_id(0)
    first, second = bounds_ref[0], bounds_ref[1]
    rows = q_ref.shape[0]
    width = local_heads * HEAD_DIM
    k_row = lax.broadcasted_iota(jnp.int32, (block, block), 0)
    q_col = lax.broadcasted_iota(jnp.int32, (1, block), 1)
    for i in range(rows // block):
        part = pl.ds(i * block, block)
        product = grad_ref[part, :].astype(jnp.float32) * context_ref[part, :].astype(jnp.float32)
        inner_ref[:, part] = jnp.sum(jnp.transpose(product), axis=0, keepdims=True)
    query_acc[...] = jnp.zeros_like(query_acc)

    def key_step(key_block, _):
        base = pl.multiple_of(key_block * block, block)
        key_rows = pl.ds(base, block)
        key_acc[...] = jnp.zeros_like(key_acc)
        value_acc[...] = jnp.zeros_like(value_acc)

        def query_step(query_block, _):
            offset = pl.multiple_of(query_block * block, block)
            query_rows = pl.ds(offset, block)
            k = k_ref[key_rows, :]
            q = q_ref[query_rows, :]
            grad = grad_ref[query_rows, :]
            q_pos = offset + q_col
            start = segment_start(q_pos, first, second)
            scores = dot(k, q, ((1,), (1,)))
            allowed = (k_row <= q_pos - base) & (k_row >= start - base)
            exponent = jnp.where(
                allowed, scores * SCALE_LOG2 - total_ref[0, :, query_rows], MASKED
            )
            weights = jnp.exp2(exponent)
            grad_weights = dot(v_ref[key_rows, :], grad, ((1,), (1,)))
            score_grad = (weights * (grad_weights - inner_ref[:, query_rows])).astype(jnp.bfloat16)
            value_acc[...] += dot(weights.astype(jnp.bfloat16), grad, ((1,), (0,)))
            key_acc[...] += dot(score_grad, q, ((1,), (0,)))
            query_acc[query_rows, :] += dot(score_grad, k, ((0,), (0,)))
            return 0

        last = segment_end(base + block - 1, first, second, rows) - 1
        lax.fori_loop(key_block, last // block + 1, query_step, 0)
        key_columns = pl.ds(pl.multiple_of(width + head * HEAD_DIM, HEAD_DIM), HEAD_DIM)
        value_columns = pl.ds(pl.multiple_of(2 * width + head * HEAD_DIM, HEAD_DIM), HEAD_DIM)
        out_ref[key_rows, key_columns] = (key_acc[...] * SCALE).astype(jnp.bfloat16)
        out_ref[key_rows, value_columns] = value_acc[...].astype(jnp.bfloat16)
        return 0

    lax.fori_loop(0, rows // block, key_step, 0)
    query_columns = pl.ds(pl.multiple_of(head * HEAD_DIM, HEAD_DIM), HEAD_DIM)
    out_ref[:, query_columns] = (query_acc[...] * SCALE).astype(jnp.bfloat16)


def attend_back(bounds, projected, grad_context, context, totals, local_heads):
    rows = projected.shape[0]
    block = min(BLOCK, rows)
    width = local_heads * HEAD_DIM
    column = pl.BlockSpec((rows, HEAD_DIM), lambda h, _: (0, h))
    return pl.pallas_call(
        functools.partial(attend_back_kernel, block, local_heads),
        grid_spec=pltpu.PrefetchScalarGridSpec(
            num_scalar_prefetch=1,
            grid=(local_heads,),
            in_specs=[
                column,
                pl.BlockSpec((rows, HEAD_DIM), lambda h, _: (0, local_heads + h)),
                pl.BlockSpec((rows, HEAD_DIM), lambda h, _: (0, 2 * local_heads + h)),
                column,
                column,
                pl.BlockSpec((1, 1, rows), lambda h, _: (h, 0, 0)),
            ],
            out_specs=pl.BlockSpec((rows, 3 * width), lambda h, _: (0, 0)),
            scratch_shapes=[
                pltpu.VMEM((rows, HEAD_DIM), jnp.float32),
                pltpu.VMEM((block, HEAD_DIM), jnp.float32),
                pltpu.VMEM((block, HEAD_DIM), jnp.float32),
                pltpu.VMEM((1, rows), jnp.float32),
            ],
        ),
        out_shape=jax.ShapeDtypeStruct((rows, 3 * width), jnp.bfloat16),
        compiler_params=pltpu.CompilerParams(vmem_limit_bytes=VMEM_LIMIT),
        cost_estimate=pl.CostEstimate(
            flops=10 * local_heads * rows * rows * HEAD_DIM,
            bytes_accessed=16 * rows * width,
            transcendentals=local_heads * rows * rows,
        ),
    )(bounds, projected, projected, projected, grad_context, context, totals)


def normalize(values):
    center = values - jnp.mean(values, axis=-1, keepdims=True)
    inverse = lax.rsqrt(jnp.mean(center * center, axis=-1, keepdims=True) + EPSILON)
    return center * inverse, inverse


def normalize_back(grad, gain, unit, inverse):
    scaled = grad * gain
    return inverse * (
        scaled
        - jnp.mean(scaled, axis=-1, keepdims=True)
        - unit * jnp.mean(scaled * unit, axis=-1, keepdims=True)
    )


def gelu_tanh(values):
    return jax.nn.gelu(values, approximate=True)


def after(value, *earlier):
    return lax.optimization_barrier((value,) + earlier)[0]


def ring_order(chips):
    return [c for c in range(chips) if c == 0 or c % 2] + [
        c for c in reversed(range(2, chips)) if c % 2 == 0
    ]


def ring_step(value):
    size = lax.axis_size("tensor")
    order = ring_order(size // 2)
    pairs = []
    for place, chip in enumerate(order):
        following = order[(place + 1) % len(order)]
        pairs += [(2 * chip, 2 * following), (2 * chip + 1, 2 * following + 1)]
    return lax.ppermute(value, "tensor", pairs)


def swap_cores(value):
    return lax.ppermute(value, "tensor", [(i, i ^ 1) for i in range(lax.axis_size("tensor"))])


def ring_chip(step):
    chips = lax.axis_size("tensor") // 2
    order = ring_order(chips)
    places = jnp.array([order.index(c) for c in range(chips)], jnp.int32)
    place = places[lax.axis_index("tensor") // 2]
    return jnp.array(order, jnp.int32)[(place + chips - step) % chips]


def ring_gather(block):
    moving = block
    pairs = []
    for step in range(lax.axis_size("tensor") // 2):
        if step:
            moving = ring_step(moving)
        pairs.append((moving, swap_cores(moving)))
    return pairs


def ring_scatter(part, ties=()):
    arrivals = []
    chips = lax.axis_size("tensor") // 2
    for step in list(range(1, chips)) + [0]:
        mine, other = part(step)
        total = mine.astype(jnp.float32) + swap_cores(other).astype(jnp.float32)
        if arrivals:
            total = total + arrivals[-1].astype(jnp.float32)
        if step:
            arrived = ring_step(total.astype(jnp.bfloat16))
            if len(arrivals) < len(ties):
                arrived = after(arrived, *ties[len(arrivals)])
            arrivals.append(arrived)
    return total, arrivals


def in_order(pairs):
    size = lax.axis_size("tensor")
    core = lax.axis_index("tensor") % 2
    block = pairs[0][0]
    full = jnp.zeros((size,) + block.shape, block.dtype)
    for step, (mine, other) in enumerate(pairs):
        chip = ring_chip(step)
        full = lax.dynamic_update_index_in_dim(full, mine, 2 * chip + core, 0)
        full = lax.dynamic_update_index_in_dim(full, other, 2 * chip + 1 - core, 0)
    return full


def flip_dp(value, bit):
    size = lax.axis_size("dp")
    return lax.ppermute(value, "dp", [(i, i ^ bit) for i in range(size)])


def dp_bits():
    return [1 << i for i in range((lax.axis_size("dp") - 1).bit_length())]


def tied(ties):
    left = list(ties)

    def tie(value):
        return after(value, *left.pop(0)) if left else value

    return tie


def dp_halves(value, bits, axis, ties):
    tie = tied(ties)
    me = lax.axis_index("dp")
    stages = [value]
    for bit in bits:
        half = value.shape[axis] // 2
        up = (me & bit) != 0
        keep = lax.dynamic_slice_in_dim(value, jnp.where(up, half, 0), half, axis)
        give = lax.dynamic_slice_in_dim(value, jnp.where(up, 0, half), half, axis)
        got = tie(flip_dp(give, bit))
        value = (keep.astype(jnp.float32) + got.astype(jnp.float32)).astype(value.dtype)
        stages.append(value)
    return stages


def dp_blocks(value, bits, ties):
    tie = tied(ties)
    blocks = [(0, value)]
    first = None
    for bit in bits:
        got = tie(flip_dp(jnp.concatenate([block for _, block in blocks], axis=0), bit))
        first = got if first is None else first
        blocks += [
            (mask ^ bit, piece) for (mask, _), piece in zip(blocks, jnp.split(got, len(blocks)))
        ]
    return blocks, first


def cut_place(mask, bits, size):
    device = lax.axis_index("dp") ^ mask
    place = 0
    for bit in bits:
        size //= 2
        place = place + jnp.where((device & bit) != 0, size, 0)
    return place


def put(full, block, rows, column=0):
    block = block.astype(full.dtype).reshape(block.shape[:1] + full.shape[1:2] + (-1,)) if full.ndim == 3 else block.astype(full.dtype)
    return lax.dynamic_update_slice(full, block, (rows, column) + (0,) * (full.ndim - 2))


def small_sum(value, axes):
    for axis in axes:
        size = lax.axis_size(axis)
        bit = 1
        while bit < size:
            value = value + lax.ppermute(value, axis, [(i, i ^ bit) for i in range(size)])
            bit *= 2
    return value


def shards(
    tokens,
    lengths,
    attention_gain,
    attention_shift,
    query_key_value,
    query_value_bias,
    output_weight,
    output_bias,
    feedforward_gain,
    feedforward_shift,
    expand_weight,
    expand_bias,
    contract_weight,
    contract_bias,
    cotangent,
):
    bf16, f32 = jnp.bfloat16, jnp.float32
    shard_rows, features = tokens.shape
    tensor_size = lax.axis_size("tensor")
    group_count = lax.axis_size("dp")
    group = lax.axis_index("dp")
    rank = lax.axis_index("tensor")
    core = rank % 2
    chips = tensor_size // 2
    group_rows = shard_rows * tensor_size
    local_width = query_key_value.shape[2]
    local_heads = local_width // HEAD_DIM
    bounds = jnp.cumsum(lengths, axis=1)
    own_bounds = lax.dynamic_index_in_dim(bounds, group, 0, keepdims=False)
    own_count = own_bounds[-1]
    share = own_count.astype(f32) / jnp.sum(bounds[:, -1]).astype(f32)
    local_rows = rank * shard_rows + jnp.arange(shard_rows, dtype=jnp.int32)
    local_live = (local_rows < own_count).astype(f32)[:, None]

    def dot(a, b, a_axis, b_axis):
        return lax.dot_general(
            a, b, (((a_axis,), (b_axis,)), ((), ())), preferred_element_type=jnp.float32
        )

    def chip_rows(rows, step):
        first = ring_chip(step) * 2 * shard_rows
        return jnp.concatenate(
            [
                lax.dynamic_slice_in_dim(rows, first + core * shard_rows, shard_rows),
                lax.dynamic_slice_in_dim(rows, first + (1 - core) * shard_rows, shard_rows),
            ],
            axis=0,
        )

    def ordered(blocks):
        return in_order([(b[:shard_rows], b[shard_rows:]) for b in blocks]).reshape(
            group_rows, blocks[0].shape[1]
        )

    input_rows = tokens.astype(f32)
    unit_one, inverse_one = normalize(input_rows)
    normed_rows = (unit_one * attention_gain + attention_shift).astype(bf16)
    normed = lax.all_gather(normed_rows, "tensor", axis=0, tiled=True)

    columns = features // group_count
    moving = lax.dynamic_slice_in_dim(output_weight, group * columns, columns, 1)
    pieces = [moving]
    for _ in range(1, chips):
        with jax.named_scope("weight_ring"):
            moving = ring_step(moving)
        pieces.append(moving)
    bits = dp_bits()
    pieces = jnp.concatenate(pieces, axis=0)
    half = pieces.shape[0] // 2

    weight_own = jnp.zeros((2 * half, features), bf16)
    with jax.named_scope("weight_dp"):
        for start, order in ((0, bits), (half, bits[::-1])):
            for mask, block in dp_blocks(pieces[start : start + half], order, [])[0]:
                weight_own = put(weight_own, block, start, (group ^ mask) * columns)
    weight_other = swap_cores(weight_own)

    weight_flat = query_key_value.reshape(features, 3 * local_width)
    bias_flat = jnp.concatenate(
        [query_value_bias[0], jnp.zeros_like(query_value_bias[0]), query_value_bias[1]]
    )
    normed, weight_own, weight_other, weight_flat = lax.optimization_barrier(
        (normed, weight_own, weight_other, weight_flat)
    )
    grad_rows_low = jnp.where(local_live > 0, cotangent, jnp.zeros_like(cotangent))
    grad_out = lax.all_gather(after(grad_rows_low, normed), "tensor", axis=0, tiled=True)

    projected = (dot(normed, weight_flat, 1, 0) + bias_flat).astype(bf16)
    context, totals = attend(own_bounds, projected, local_heads)

    arrived = lax.all_to_all(
        context.reshape(tensor_size, shard_rows, local_width), "tensor", 0, 0, tiled=True
    )

    def heads_of(parity):
        return jnp.concatenate(
            [
                lax.dynamic_index_in_dim(arrived, 2 * ring_chip(step) + parity, 0, False)
                for step in range(chips)
            ],
            axis=1,
        )

    context_own, context_other = heads_of(core), heads_of(1 - core)
    hidden = (
        input_rows
        + dot(context_own, weight_own, 1, 0)
        + dot(context_other, weight_other, 1, 0)
        + output_bias
    )
    unit_two, inverse_two = normalize(hidden)
    mixed_rows = (unit_two * feedforward_gain + feedforward_shift).astype(bf16)

    mixed, activated, grad_pre, mixed_terms, mixed_arrivals = [], [], [], [], []
    moving = after(mixed_rows, grad_out)

    def mixed_step(step):
        mixed.append(jnp.concatenate([moving, swap_cores(moving)], axis=0))
        rows = mixed[step]
        if step > 2:
            rows = after(rows, mixed_arrivals[step - 3])
        grad_activated = dot(chip_rows(grad_out, step), contract_weight, 1, 1)
        pre_act = dot(rows, expand_weight, 1, 0) + expand_bias
        value, gelu_pull = jax.vjp(gelu_tanh, pre_act)
        activated.append(value.astype(bf16))
        grad_pre.append(gelu_pull(grad_activated)[0].astype(bf16))
        mixed_terms.append(dot(grad_pre[step], expand_weight, 1, 1).astype(bf16))

    def chip_total(terms, arrivals):
        total = terms[:shard_rows].astype(f32) + swap_cores(terms[shard_rows:]).astype(f32)
        return total + arrivals[-1].astype(f32) if arrivals else total

    for step in range(chips):
        with jax.named_scope(f"mixed_ring{step}"):
            if step:
                moving = ring_step(moving if step < 3 else after(moving, mixed_terms[step - 2]))
            mixed_step(step)
        if step:
            with jax.named_scope(f"grad_mixed_ring{step}"):
                total = chip_total(mixed_terms[step], mixed_arrivals)
                mixed_arrivals.append(ring_step(total.astype(bf16)))
    second = mixed_arrivals[-2]
    activated_all = after(ordered(activated), second)
    grad_pre_all = after(ordered(grad_pre), second)
    mixed_all = ordered(mixed)
    with jax.named_scope("contract_gradient"):
        contract_local = (share * dot(activated_all, grad_out, 0, 0)).astype(bf16)
    with jax.named_scope("expand_gradient"):
        expand_local = (share * dot(mixed_all, grad_pre_all, 0, 0)).astype(bf16)
    mixed_arrivals[-1] = after(mixed_arrivals[-1], contract_local, expand_local)
    with jax.named_scope("grad_mixed_own"):
        grad_mixed = chip_total(mixed_terms[0], mixed_arrivals)

    grad_local = grad_rows_low.astype(f32)
    grad_hidden = grad_local + normalize_back(grad_mixed, feedforward_gain, unit_two, inverse_two)
    grad_hidden_low = grad_hidden.astype(bf16)
    with jax.named_scope("grad_hidden_gather"):
        grad_hidden_all = lax.all_gather(grad_hidden_low, "tensor", axis=0, tiled=True)

    with jax.named_scope("contract_dp"):
        contract_half = dp_halves(contract_local, bits[:1], 0, [(grad_hidden_low,)])[-1]
        contract_cut = dp_halves(contract_half, bits[1:], 0, [(grad_hidden_all,)])[-1]
    with jax.named_scope("expand_dp"):
        expand_half = dp_halves(expand_local, bits[::-1][:1], 0, [(grad_hidden_low,)])[-1]
        expand_cut = dp_halves(expand_half, bits[::-1][1:], 0, [(grad_hidden_all,)])[-1]
    grad_hidden_all = after(grad_hidden_all, contract_cut, expand_cut)
    with jax.named_scope("grad_context"):
        grad_context = dot(grad_hidden_all, output_weight, 1, 1).astype(bf16)

    branch_terms = [
        dot(after(block, grad_hidden_low), contract_weight, 1, 0).astype(bf16) for block in activated
    ]

    def branch_part(step):
        block = after(branch_terms[step], grad_hidden_all)
        return block[:shard_rows], block[shard_rows:]

    def branch_total(step):
        mine, other = branch_part(step)
        return mine.astype(f32) + swap_cores(other).astype(f32)

    with jax.named_scope("branch_ring1"):
        branch_arrived = ring_step(branch_total(1).astype(bf16))

    with jax.named_scope("output_gradient"):
        output_local = (share * dot(context, grad_hidden_all, 0, 0)).astype(bf16)
    with jax.named_scope("output_dp"):
        output_gradient = lax.psum(output_local, "dp")
    projected_grad = attend_back(own_bounds, projected, grad_context, context, totals, local_heads)
    projected_grad, branch_arrived = lax.optimization_barrier((projected_grad, branch_arrived))

    normed_terms = []
    with jax.named_scope("normed_terms"):
        for step in range(chips):
            rows = lax.dynamic_slice_in_dim(
                projected_grad, ring_chip(step) * 2 * shard_rows, 2 * shard_rows
            )
            normed_terms.append(dot(rows, weight_flat, 1, 1).astype(bf16))
    projected_late = after(projected_grad, *normed_terms)
    with jax.named_scope("projection_gradient"):
        projection_local = (share * dot(normed, projected_late, 0, 0)).astype(bf16)

    def normed_total(step):
        mine = lax.dynamic_slice_in_dim(normed_terms[step], core * shard_rows, shard_rows)
        other = lax.dynamic_slice_in_dim(normed_terms[step], (1 - core) * shard_rows, shard_rows)
        return mine.astype(f32) + swap_cores(other).astype(f32)


    normed_arrivals = []

    def normed_step(step, *meanwhile):
        total = normed_total(step)
        if normed_arrivals:
            total = total + after(normed_arrivals[-1], *meanwhile).astype(f32)
        with jax.named_scope(f"grad_normed_ring{step}"):
            normed_arrivals.append(ring_step(total.astype(bf16)))

    with jax.named_scope("contract_dp"):
        contract_blocks, contract_first = dp_blocks(
            contract_cut, bits[::-1], [(projected_late,), (projected_late,)]
        )
    with jax.named_scope("expand_dp"):
        expand_blocks, expand_first = dp_blocks(
            expand_cut, bits, [(projected_late,), (projected_late,)]
        )
    for step in range(1, chips):
        normed_step(step, *((contract_first, expand_first) if step == 2 else ()))
    last = normed_arrivals[-1]
    with jax.named_scope("projection_dp"):
        projection_gradient = lax.psum(
            after(projection_local, normed_arrivals[0], output_gradient), "dp"
        )
    projection_gradient = projection_gradient.reshape(features, 3, local_width).astype(f32)
    output_gradient = output_gradient.astype(f32)
    with jax.named_scope("grad_normed_own"):
        grad_normed = normed_total(0) + last.astype(f32)

    branch_arrived = after(branch_arrived, last)
    for step in range(2, chips):
        with jax.named_scope(f"branch_ring{step}"):
            total = branch_total(step) + branch_arrived.astype(f32)
            branch_arrived = ring_step(total.astype(bf16))
    with jax.named_scope("branch_own"):
        branch = branch_total(0) + branch_arrived.astype(f32)
    layer_output = (local_live * (hidden + branch + contract_bias)).astype(bf16)
    input_gradient = (
        grad_hidden + normalize_back(grad_normed, attention_gain, unit_one, inverse_one)
    ).astype(bf16)

    contract_gradient = jnp.zeros(contract_local.shape, f32)
    for mask, block in contract_blocks:
        contract_gradient = put(
            contract_gradient, after(block, last), cut_place(mask, bits, contract_local.shape[0])
        )
    expand_gradient = jnp.zeros(expand_local.shape, f32)
    for mask, block in expand_blocks:
        expand_gradient = put(
            expand_gradient, after(block, last), cut_place(mask, bits[::-1], expand_local.shape[0])
        )
    sums_by_row = share * jnp.stack(
        [
            jnp.sum(grad_normed * unit_one, axis=0),
            jnp.sum(grad_normed, axis=0),
            jnp.sum(grad_hidden, axis=0),
            jnp.sum(grad_mixed * unit_two, axis=0),
            jnp.sum(grad_mixed, axis=0),
            jnp.sum(grad_local, axis=0),
        ]
    )
    column_sums = jnp.sum(projected_grad.astype(f32), axis=0)
    sums_by_width = share * jnp.concatenate(
        [
            column_sums[:local_width],
            column_sums[2 * local_width :],
            jnp.sum(grad_pre_all.astype(f32), axis=0),
        ]
    )
    own_columns = features // tensor_size
    with jax.named_scope("small_sums"):
        sums_by_row = small_sum(sums_by_row, ("tensor",))
        sums_by_row = lax.dynamic_slice_in_dim(sums_by_row, rank * own_columns, own_columns, 1)
        sums = small_sum(jnp.concatenate([sums_by_row.reshape(-1), sums_by_width]), ("dp",))
    sums_by_row = sums[: 6 * own_columns].reshape(6, own_columns)
    sums_by_width = sums[6 * own_columns :]
    query_value_gradient = sums_by_width[: 2 * local_width].reshape(2, local_width)
    expand_bias_gradient = sums_by_width[2 * local_width :]
    return (
        layer_output,
        input_gradient,
        sums_by_row[0],
        sums_by_row[1],
        projection_gradient,
        query_value_gradient,
        output_gradient,
        sums_by_row[2],
        sums_by_row[3],
        sums_by_row[4],
        expand_gradient,
        expand_bias_gradient,
        contract_gradient,
        sums_by_row[5],
    )


def solution(mesh):
    placed = (
        P(("dp", "tensor"), None),
        P(),
        P(),
        P(),
        P(None, None, "tensor"),
        P(None, "tensor"),
        P("tensor", None),
        P(),
        P(),
        P(),
        P(None, "tensor"),
        P("tensor"),
        P("tensor", None),
        P(),
        P(("dp", "tensor"), None),
    )
    return jax.shard_map(
        shards,
        mesh=mesh,
        in_specs=placed,
        out_specs=(
            P(("dp", "tensor"), None),
            P(("dp", "tensor"), None),
            P("tensor"),
            P("tensor"),
            P(None, None, "tensor"),
            P(None, "tensor"),
            P("tensor", None),
            P("tensor"),
            P("tensor"),
            P("tensor"),
            P(None, "tensor"),
            P("tensor"),
            P("tensor", None),
            P("tensor"),
        ),
        check_vma=False,
    )
```

```python
import functools
import math

import jax
import jax.numpy as jnp
from jax import lax
from jax.experimental import pallas as pl
from jax.experimental.pallas import tpu as pltpu
from jax.sharding import PartitionSpec as P

HEAD_DIM = 128
BLOCK = 512
EPSILON = 1e-05
SCALE = HEAD_DIM ** (-0.5)
SCALE_LOG2 = SCALE * math.log2(math.e)
MASKED = -1e30
VMEM_LIMIT = 48 * 1024 * 1024


def dot(a, b, contract):
    return lax.dot_general(a, b, (contract, ((), ())), preferred_element_type=jnp.float32)


def segment_start(position, first, second):
    return jnp.where(position >= second, second, jnp.where(position >= first, first, 0))


def segment_end(position, first, second, rows):
    return jnp.where(position >= second, rows, jnp.where(position >= first, second, first))


def attend_kernel(block, bounds_ref, q_ref, k_ref, v_ref, out_ref, total_ref):
    query_block = pl.program_id(1)
    first, second = bounds_ref[0], bounds_ref[1]
    offset = query_block * block
    q = q_ref[...]
    q_pos = offset + lax.broadcasted_iota(jnp.int32, (1, block), 1)
    start = segment_start(q_pos, first, second)
    k_row = lax.broadcasted_iota(jnp.int32, (block, block), 0)

    def step(key_block, carry):
        highest, row_sum, acc = carry
        rows = pl.ds(pl.multiple_of(key_block * block, block), block)
        scores = dot(k_ref[rows, :], q, ((1,), (1,)))
        base = key_block * block
        allowed = (k_row <= q_pos - base) & (k_row >= start - base)
        scores = jnp.where(allowed, scores * SCALE_LOG2, MASKED)
        new_highest = jnp.maximum(highest, jnp.max(scores, axis=0, keepdims=True))
        weights = jnp.exp2(scores - new_highest)
        decay = jnp.exp2(highest - new_highest)
        row_sum = row_sum * decay + jnp.sum(weights, axis=0, keepdims=True)
        acc = acc * decay + dot(v_ref[rows, :], weights.astype(jnp.bfloat16), ((0,), (0,)))
        return new_highest, row_sum, acc

    low = segment_start(offset, first, second) // block
    highest, row_sum, acc = lax.fori_loop(
        low,
        query_block + 1,
        step,
        (
            jnp.full((1, block), MASKED, jnp.float32),
            jnp.zeros((1, block), jnp.float32),
            jnp.zeros((HEAD_DIM, block), jnp.float32),
        ),
    )
    out_ref[...] = jnp.transpose(acc / row_sum).astype(jnp.bfloat16)
    total_ref[0] = highest + jnp.log2(row_sum)


def attend(bounds, projected, local_heads):
    rows = projected.shape[0]
    block = min(BLOCK, rows)
    return pl.pallas_call(
        functools.partial(attend_kernel, block),
        grid_spec=pltpu.PrefetchScalarGridSpec(
            num_scalar_prefetch=1,
            grid=(local_heads, rows // block),
            in_specs=[
                pl.BlockSpec((block, HEAD_DIM), lambda h, i, _: (i, h)),
                pl.BlockSpec((rows, HEAD_DIM), lambda h, i, _: (0, local_heads + h)),
                pl.BlockSpec((rows, HEAD_DIM), lambda h, i, _: (0, 2 * local_heads + h)),
            ],
            out_specs=[
                pl.BlockSpec((block, HEAD_DIM), lambda h, i, _: (i, h)),
                pl.BlockSpec((1, 1, block), lambda h, i, _: (h, 0, i)),
            ],
        ),
        out_shape=[
            jax.ShapeDtypeStruct((rows, local_heads * HEAD_DIM), jnp.bfloat16),
            jax.ShapeDtypeStruct((local_heads, 1, rows), jnp.float32),
        ],
        compiler_params=pltpu.CompilerParams(vmem_limit_bytes=VMEM_LIMIT),
        cost_estimate=pl.CostEstimate(
            flops=4 * local_heads * rows * rows * HEAD_DIM,
            bytes_accessed=8 * rows * local_heads * HEAD_DIM,
            transcendentals=local_heads * rows * rows,
        ),
    )(bounds, projected, projected, projected)


def attend_back_kernel(
    block,
    local_heads,
    bounds_ref,
    q_ref,
    k_ref,
    v_ref,
    grad_ref,
    context_ref,
    total_ref,
    out_ref,
    query_acc,
    key_acc,
    value_acc,
    inner_ref,
):
    head = pl.program_id(0)
    first, second = bounds_ref[0], bounds_ref[1]
    rows = q_ref.shape[0]
    width = local_heads * HEAD_DIM
    k_row = lax.broadcasted_iota(jnp.int32, (block, block), 0)
    q_col = lax.broadcasted_iota(jnp.int32, (1, block), 1)
    for i in range(rows // block):
        part = pl.ds(i * block, block)
        product = grad_ref[part, :].astype(jnp.float32) * context_ref[part, :].astype(jnp.float32)
        inner_ref[:, part] = jnp.sum(jnp.transpose(product), axis=0, keepdims=True)
    query_acc[...] = jnp.zeros_like(query_acc)

    def key_step(key_block, _):
        base = pl.multiple_of(key_block * block, block)
        key_rows = pl.ds(base, block)
        key_acc[...] = jnp.zeros_like(key_acc)
        value_acc[...] = jnp.zeros_like(value_acc)

        def query_step(query_block, _):
            offset = pl.multiple_of(query_block * block, block)
            query_rows = pl.ds(offset, block)
            k = k_ref[key_rows, :]
            q = q_ref[query_rows, :]
            grad = grad_ref[query_rows, :]
            q_pos = offset + q_col
            start = segment_start(q_pos, first, second)
            scores = dot(k, q, ((1,), (1,)))
            allowed = (k_row <= q_pos - base) & (k_row >= start - base)
            exponent = jnp.where(
                allowed, scores * SCALE_LOG2 - total_ref[0, :, query_rows], MASKED
            )
            weights = jnp.exp2(exponent)
            grad_weights = dot(v_ref[key_rows, :], grad, ((1,), (1,)))
            score_grad = (weights * (grad_weights - inner_ref[:, query_rows])).astype(jnp.bfloat16)
            value_acc[...] += dot(weights.astype(jnp.bfloat16), grad, ((1,), (0,)))
            key_acc[...] += dot(score_grad, q, ((1,), (0,)))
            query_acc[query_rows, :] += dot(score_grad, k, ((0,), (0,)))
            return 0

        last = segment_end(base + block - 1, first, second, rows) - 1
        lax.fori_loop(key_block, last // block + 1, query_step, 0)
        key_columns = pl.ds(pl.multiple_of(width + head * HEAD_DIM, HEAD_DIM), HEAD_DIM)
        value_columns = pl.ds(pl.multiple_of(2 * width + head * HEAD_DIM, HEAD_DIM), HEAD_DIM)
        out_ref[key_rows, key_columns] = (key_acc[...] * SCALE).astype(jnp.bfloat16)
        out_ref[key_rows, value_columns] = value_acc[...].astype(jnp.bfloat16)
        return 0

    lax.fori_loop(0, rows // block, key_step, 0)
    query_columns = pl.ds(pl.multiple_of(head * HEAD_DIM, HEAD_DIM), HEAD_DIM)
    out_ref[:, query_columns] = (query_acc[...] * SCALE).astype(jnp.bfloat16)


def attend_back(bounds, projected, grad_context, context, totals, local_heads):
    rows = projected.shape[0]
    block = min(BLOCK, rows)
    width = local_heads * HEAD_DIM
    column = pl.BlockSpec((rows, HEAD_DIM), lambda h, _: (0, h))
    return pl.pallas_call(
        functools.partial(attend_back_kernel, block, local_heads),
        grid_spec=pltpu.PrefetchScalarGridSpec(
            num_scalar_prefetch=1,
            grid=(local_heads,),
            in_specs=[
                column,
                pl.BlockSpec((rows, HEAD_DIM), lambda h, _: (0, local_heads + h)),
                pl.BlockSpec((rows, HEAD_DIM), lambda h, _: (0, 2 * local_heads + h)),
                column,
                column,
                pl.BlockSpec((1, 1, rows), lambda h, _: (h, 0, 0)),
            ],
            out_specs=pl.BlockSpec((rows, 3 * width), lambda h, _: (0, 0)),
            scratch_shapes=[
                pltpu.VMEM((rows, HEAD_DIM), jnp.float32),
                pltpu.VMEM((block, HEAD_DIM), jnp.float32),
                pltpu.VMEM((block, HEAD_DIM), jnp.float32),
                pltpu.VMEM((1, rows), jnp.float32),
            ],
        ),
        out_shape=jax.ShapeDtypeStruct((rows, 3 * width), jnp.bfloat16),
        compiler_params=pltpu.CompilerParams(vmem_limit_bytes=VMEM_LIMIT),
        cost_estimate=pl.CostEstimate(
            flops=10 * local_heads * rows * rows * HEAD_DIM,
            bytes_accessed=16 * rows * width,
            transcendentals=local_heads * rows * rows,
        ),
    )(bounds, projected, projected, projected, grad_context, context, totals)


def normalize(values):
    center = values - jnp.mean(values, axis=-1, keepdims=True)
    inverse = lax.rsqrt(jnp.mean(center * center, axis=-1, keepdims=True) + EPSILON)
    return center * inverse, inverse


def normalize_back(grad, gain, unit, inverse):
    scaled = grad * gain
    return inverse * (
        scaled
        - jnp.mean(scaled, axis=-1, keepdims=True)
        - unit * jnp.mean(scaled * unit, axis=-1, keepdims=True)
    )


def gelu_tanh(values):
    return jax.nn.gelu(values, approximate=True)


def after(value, *earlier):
    return lax.optimization_barrier((value,) + earlier)[0]


def ring_order(chips):
    return [c for c in range(chips) if c == 0 or c % 2] + [
        c for c in reversed(range(2, chips)) if c % 2 == 0
    ]


def ring_step(value):
    size = lax.axis_size("tensor")
    order = ring_order(size // 2)
    pairs = []
    for place, chip in enumerate(order):
        following = order[(place + 1) % len(order)]
        pairs += [(2 * chip, 2 * following), (2 * chip + 1, 2 * following + 1)]
    return lax.ppermute(value, "tensor", pairs)


def swap_cores(value):
    return lax.ppermute(value, "tensor", [(i, i ^ 1) for i in range(lax.axis_size("tensor"))])


def ring_chip(step):
    chips = lax.axis_size("tensor") // 2
    order = ring_order(chips)
    places = jnp.array([order.index(c) for c in range(chips)], jnp.int32)
    place = places[lax.axis_index("tensor") // 2]
    return jnp.array(order, jnp.int32)[(place + chips - step) % chips]


def ring_gather(block):
    moving = block
    pairs = []
    for step in range(lax.axis_size("tensor") // 2):
        if step:
            moving = ring_step(moving)
        pairs.append((moving, swap_cores(moving)))
    return pairs


def ring_scatter(part, ties=()):
    arrivals = []
    chips = lax.axis_size("tensor") // 2
    for step in list(range(1, chips)) + [0]:
        mine, other = part(step)
        total = mine.astype(jnp.float32) + swap_cores(other).astype(jnp.float32)
        if arrivals:
            total = total + arrivals[-1].astype(jnp.float32)
        if step:
            arrived = ring_step(total.astype(jnp.bfloat16))
            if len(arrivals) < len(ties):
                arrived = after(arrived, *ties[len(arrivals)])
            arrivals.append(arrived)
    return total, arrivals


def in_order(pairs):
    size = lax.axis_size("tensor")
    core = lax.axis_index("tensor") % 2
    block = pairs[0][0]
    full = jnp.zeros((size,) + block.shape, block.dtype)
    for step, (mine, other) in enumerate(pairs):
        chip = ring_chip(step)
        full = lax.dynamic_update_index_in_dim(full, mine, 2 * chip + core, 0)
        full = lax.dynamic_update_index_in_dim(full, other, 2 * chip + 1 - core, 0)
    return full


def flip_dp(value, bit):
    size = lax.axis_size("dp")
    return lax.ppermute(value, "dp", [(i, i ^ bit) for i in range(size)])


def dp_bits():
    return [1 << i for i in range((lax.axis_size("dp") - 1).bit_length())]


def sum_job(value, bits, axis=0):
    me = lax.axis_index("dp")
    for bit in bits:
        half = value.shape[axis] // 2
        up = (me & bit) != 0
        keep = lax.dynamic_slice_in_dim(value, jnp.where(up, half, 0), half, axis)
        give = lax.dynamic_slice_in_dim(value, jnp.where(up, 0, half), half, axis)
        (got,) = yield [(give, bit)]
        value = (keep.astype(jnp.float32) + got.astype(jnp.float32)).astype(value.dtype)
    blocks = [(0, value)]
    wave = [(0, value, bits[::-1])]
    while wave:
        sends = [
            (mask ^ bit, block, bit, left[place + 1 :])
            for mask, block, left in wave
            for place, bit in enumerate(left)
        ]
        if not sends:
            break
        got = yield [(block, bit) for _, block, bit, _ in sends]
        wave = [(mask, block, left) for (mask, _, _, left), block in zip(sends, got)]
        blocks += [(mask, block) for mask, block, _ in wave]
    return blocks


class Exchange:
    def __init__(self):
        self.jobs = {}
        self.done = {}
        self.flying = {}

    def add(self, name, job):
        self.jobs[name] = job
        self._advance(name, None)

    def _advance(self, name, got):
        try:
            sends = self.jobs[name].send(got)
        except StopIteration as stop:
            self.done[name] = stop.value
            del self.jobs[name]
            return
        with jax.named_scope("dp_" + name):
            self.flying[name] = [flip_dp(value, bit) for value, bit in sends]

    def hop(self, *ties):
        names = list(self.flying)
        flat = [value for name in names for value in self.flying[name]]
        flat = lax.optimization_barrier(tuple(flat) + ties)
        place = 0
        for name in names:
            count = len(self.flying.pop(name))
            self._advance(name, list(flat[place : place + count]))
            place += count
        return flat[place:] if len(ties) != 1 else flat[-1]


def dp_blocks(value, bits, ties):
    blocks = [(0, value, 0)]
    for bit in bits:
        for mask, block, hops in list(blocks):
            got = flip_dp(block, bit)
            if hops < len(ties):
                got = after(got, *ties[hops])
            blocks.append((mask ^ bit, got, hops + 1))
    return [(mask, block) for mask, block, _ in blocks]


def cut_place(mask, bits, size):
    device = lax.axis_index("dp") ^ mask
    place = 0
    for bit in bits:
        size //= 2
        place = place + jnp.where((device & bit) != 0, size, 0)
    return place


def put(full, block, row, column=0):
    return lax.dynamic_update_slice(full, block.astype(full.dtype), (row, column))


def small_sum(value, axes):
    for axis in axes:
        size = lax.axis_size(axis)
        bit = 1
        while bit < size:
            value = value + lax.ppermute(value, axis, [(i, i ^ bit) for i in range(size)])
            bit *= 2
    return value


def shards(
    tokens,
    lengths,
    attention_gain,
    attention_shift,
    query_key_value,
    query_value_bias,
    output_weight,
    output_bias,
    feedforward_gain,
    feedforward_shift,
    expand_weight,
    expand_bias,
    contract_weight,
    contract_bias,
    cotangent,
):
    bf16, f32 = jnp.bfloat16, jnp.float32
    shard_rows, features = tokens.shape
    tensor_size = lax.axis_size("tensor")
    group_count = lax.axis_size("dp")
    group = lax.axis_index("dp")
    rank = lax.axis_index("tensor")
    core = rank % 2
    chips = tensor_size // 2
    group_rows = shard_rows * tensor_size
    local_width = query_key_value.shape[2]
    local_heads = local_width // HEAD_DIM
    bounds = jnp.cumsum(lengths, axis=1)
    own_bounds = lax.dynamic_index_in_dim(bounds, group, 0, keepdims=False)
    own_count = own_bounds[-1]
    share = own_count.astype(f32) / jnp.sum(bounds[:, -1]).astype(f32)
    local_rows = rank * shard_rows + jnp.arange(shard_rows, dtype=jnp.int32)
    local_live = (local_rows < own_count).astype(f32)[:, None]

    def dot(a, b, a_axis, b_axis):
        return lax.dot_general(
            a, b, (((a_axis,), (b_axis,)), ((), ())), preferred_element_type=jnp.float32
        )

    def chip_rows(rows, step):
        first = ring_chip(step) * 2 * shard_rows
        return jnp.concatenate(
            [
                lax.dynamic_slice_in_dim(rows, first + core * shard_rows, shard_rows),
                lax.dynamic_slice_in_dim(rows, first + (1 - core) * shard_rows, shard_rows),
            ],
            axis=0,
        )

    def ordered(blocks):
        return in_order([(b[:shard_rows], b[shard_rows:]) for b in blocks]).reshape(
            group_rows, blocks[0].shape[1]
        )

    input_rows = tokens.astype(f32)
    unit_one, inverse_one = normalize(input_rows)
    normed_rows = (unit_one * attention_gain + attention_shift).astype(bf16)
    normed = lax.all_gather(normed_rows, "tensor", axis=0, tiled=True)

    columns = features // group_count
    moving = lax.dynamic_slice_in_dim(output_weight, group * columns, columns, 1)
    pieces = [moving]
    for _ in range(1, chips):
        with jax.named_scope("weight_ring"):
            moving = ring_step(moving)
        pieces.append(moving)
    bits = dp_bits()
    pieces = jnp.concatenate(pieces, axis=0)
    half = pieces.shape[0] // 2

    weight_own = jnp.zeros((2 * half, features), bf16)
    with jax.named_scope("weight_dp"):
        for start, order in ((0, bits), (half, bits[::-1])):
            for mask, block in dp_blocks(pieces[start : start + half], order, []):
                weight_own = put(weight_own, block, start, (group ^ mask) * columns)
    weight_other = swap_cores(weight_own)

    weight_flat = query_key_value.reshape(features, 3 * local_width)
    bias_flat = jnp.concatenate(
        [query_value_bias[0], jnp.zeros_like(query_value_bias[0]), query_value_bias[1]]
    )
    normed, weight_own, weight_other, weight_flat = lax.optimization_barrier(
        (normed, weight_own, weight_other, weight_flat)
    )
    grad_rows_low = jnp.where(local_live > 0, cotangent, jnp.zeros_like(cotangent))
    grad_out = lax.all_gather(after(grad_rows_low, normed), "tensor", axis=0, tiled=True)

    projected = (dot(normed, weight_flat, 1, 0) + bias_flat).astype(bf16)
    context, totals = attend(own_bounds, projected, local_heads)

    arrived = lax.all_to_all(
        context.reshape(tensor_size, shard_rows, local_width), "tensor", 0, 0, tiled=True
    )

    def heads_of(parity):
        return jnp.concatenate(
            [
                lax.dynamic_index_in_dim(arrived, 2 * ring_chip(step) + parity, 0, False)
                for step in range(chips)
            ],
            axis=1,
        )

    context_own, context_other = heads_of(core), heads_of(1 - core)
    hidden = (
        input_rows
        + dot(context_own, weight_own, 1, 0)
        + dot(context_other, weight_other, 1, 0)
        + output_bias
    )
    unit_two, inverse_two = normalize(hidden)
    mixed_rows = (unit_two * feedforward_gain + feedforward_shift).astype(bf16)

    mixed, activated, grad_pre, mixed_terms, mixed_arrivals = [], [], [], [], []
    moving = after(mixed_rows, grad_out)

    def mixed_step(step):
        mixed.append(jnp.concatenate([moving, swap_cores(moving)], axis=0))
        rows = mixed[step]
        if step > 2:
            rows = after(rows, mixed_arrivals[step - 3])
        grad_activated = dot(chip_rows(grad_out, step), contract_weight, 1, 1)
        pre_act = dot(rows, expand_weight, 1, 0) + expand_bias
        value, gelu_pull = jax.vjp(gelu_tanh, pre_act)
        activated.append(value.astype(bf16))
        grad_pre.append(gelu_pull(grad_activated)[0].astype(bf16))
        mixed_terms.append(dot(grad_pre[step], expand_weight, 1, 1).astype(bf16))

    def chip_total(terms, arrivals):
        total = terms[:shard_rows].astype(f32) + swap_cores(terms[shard_rows:]).astype(f32)
        return total + arrivals[-1].astype(f32) if arrivals else total

    for step in range(chips):
        with jax.named_scope(f"mixed_ring{step}"):
            if step:
                moving = ring_step(moving if step < 3 else after(moving, mixed_terms[step - 2]))
            mixed_step(step)
        if step:
            with jax.named_scope(f"grad_mixed_ring{step}"):
                total = chip_total(mixed_terms[step], mixed_arrivals)
                mixed_arrivals.append(ring_step(total.astype(bf16)))
    second = mixed_arrivals[-2]
    activated_all = after(ordered(activated), second)
    grad_pre_all = after(ordered(grad_pre), second)
    mixed_all = ordered(mixed)
    with jax.named_scope("contract_gradient"):
        contract_local = (share * dot(activated_all, grad_out, 0, 0)).astype(bf16)
    with jax.named_scope("expand_gradient"):
        expand_local = (share * dot(mixed_all, grad_pre_all, 0, 0)).astype(bf16)
    mixed_arrivals[-1] = after(mixed_arrivals[-1], contract_local, expand_local)
    with jax.named_scope("grad_mixed_own"):
        grad_mixed = chip_total(mixed_terms[0], mixed_arrivals)

    grad_local = grad_rows_low.astype(f32)
    grad_hidden = grad_local + normalize_back(grad_mixed, feedforward_gain, unit_two, inverse_two)
    grad_hidden_low = grad_hidden.astype(bf16)
    with jax.named_scope("grad_hidden_gather"):
        grad_hidden_all = lax.all_gather(grad_hidden_low, "tensor", axis=0, tiled=True)

    exchange = Exchange()
    exchange.add("contract", sum_job(contract_local, bits))
    exchange.add("expand", sum_job(expand_local, bits[::-1]))
    branch_terms = [
        dot(after(block, grad_hidden_low), contract_weight, 1, 0).astype(bf16) for block in activated
    ]
    branch_totals = [
        block[:shard_rows].astype(f32) + swap_cores(block[shard_rows:]).astype(f32)
        for block in branch_terms
    ]
    branch_sent = branch_totals[1].astype(bf16)
    grad_hidden_low = exchange.hop(grad_hidden_low)
    for _ in bits[1:]:
        grad_hidden_low = exchange.hop(grad_hidden_low, *branch_terms, branch_sent)[0]
    grad_hidden_all, branch_sent = lax.optimization_barrier(
        (after(grad_hidden_all, grad_hidden_low), branch_sent)
    )
    with jax.named_scope("branch_ring1"):
        branch_arrived = ring_step(branch_sent)
    with jax.named_scope("grad_context"):
        grad_context = dot(grad_hidden_all, output_weight, 1, 1).astype(bf16)

    def branch_step(step):
        with jax.named_scope(f"branch_ring{step}"):
            total = branch_totals[step] + branch_arrived.astype(f32)
            return ring_step(total.astype(bf16))

    projected_grad = attend_back(own_bounds, projected, grad_context, context, totals, local_heads)
    projected_grad, branch_arrived = lax.optimization_barrier((projected_grad, branch_arrived))
    branch_arrived = branch_step(2)
    with jax.named_scope("normed_terms"):
        normed_terms = dot(projected_grad, weight_flat, 1, 1).astype(bf16)
    normed_terms, branch_arrived = exchange.hop(normed_terms, branch_arrived)
    projected_late = after(projected_grad, normed_terms)
    with jax.named_scope("grad_normed_scatter"):
        grad_normed = lax.psum_scatter(
            normed_terms, "tensor", scatter_dimension=0, tiled=True
        ).astype(f32)

    with jax.named_scope("projection_gradient"):
        projection_local = (share * dot(normed, projected_late, 0, 0)).astype(bf16)
    with jax.named_scope("output_gradient"):
        output_local = (share * dot(context, after(grad_hidden_all, normed_terms), 0, 0)).astype(
            bf16
        )
    cut = projection_local.shape[0] // 2
    projection_orders = ((0, bits), (cut, bits[::-1]))
    for start, order in projection_orders:
        exchange.add(f"projection{start}", sum_job(projection_local[start : start + cut], order))
    exchange.add("output", sum_job(output_local, bits))
    sums_by_row = share * jnp.stack(
        [
            jnp.sum(grad_normed * unit_one, axis=0),
            jnp.sum(grad_normed, axis=0),
            jnp.sum(grad_hidden, axis=0),
            jnp.sum(grad_mixed * unit_two, axis=0),
            jnp.sum(grad_mixed, axis=0),
            jnp.sum(grad_local, axis=0),
        ]
    )
    column_sums = jnp.sum(projected_grad.astype(f32), axis=0)
    sums_by_width = share * jnp.concatenate(
        [
            column_sums[:local_width],
            column_sums[2 * local_width :],
            jnp.sum(grad_pre_all.astype(f32), axis=0),
        ]
    )
    own_columns = features // tensor_size
    for _ in bits[1:]:
        exchange.hop()
    branch_arrived = exchange.hop(branch_arrived)
    sums_by_row, branch_arrived = lax.optimization_barrier((sums_by_row, branch_arrived))
    for step in range(3, chips):
        branch_arrived = branch_step(step)
    branch = branch_totals[0] + branch_arrived.astype(f32)
    layer_output = (local_live * (hidden + branch + contract_bias)).astype(bf16)
    exchange.hop()
    while exchange.flying:
        sums_by_row = exchange.hop(sums_by_row)
    with jax.named_scope("small_sums"):
        sums = small_sum(jnp.concatenate([sums_by_row.reshape(-1), sums_by_width]), ("dp",))
        sums_by_width = sums[sums_by_row.size :]
        sums_by_row = small_sum(
            sums[: sums_by_row.size].reshape(sums_by_row.shape), ("tensor",)
        )
        sums_by_row = lax.dynamic_slice_in_dim(sums_by_row, rank * own_columns, own_columns, 1)
    projection_parts = [
        (start, order, exchange.done[f"projection{start}"]) for start, order in projection_orders
    ]
    zero = after(jnp.zeros((), f32), normed_terms)
    input_gradient = (
        grad_hidden + normalize_back(grad_normed, attention_gain, unit_one, inverse_one)
    ).astype(bf16)

    contract_gradient = jnp.broadcast_to(zero, contract_local.shape)
    for mask, block in exchange.done["contract"]:
        contract_gradient = put(
            contract_gradient, block, cut_place(mask, bits, contract_local.shape[0])
        )
    expand_gradient = jnp.broadcast_to(zero, expand_local.shape)
    for mask, block in exchange.done["expand"]:
        expand_gradient = put(
            expand_gradient, block, cut_place(mask, bits[::-1], expand_local.shape[0])
        )
    projection_gradient = jnp.broadcast_to(zero.astype(bf16), projection_local.shape)
    for start, order, blocks in projection_parts:
        for mask, block in blocks:
            projection_gradient = put(
                projection_gradient, block, start + cut_place(mask, order, cut)
            )
    projection_gradient = projection_gradient.reshape(features, 3, local_width).astype(f32)
    output_gradient = jnp.broadcast_to(zero, output_local.shape)
    for mask, block in exchange.done["output"]:
        output_gradient = put(
            output_gradient, block, cut_place(mask, bits, output_local.shape[0])
        )

    query_value_gradient = sums_by_width[: 2 * local_width].reshape(2, local_width)
    expand_bias_gradient = sums_by_width[2 * local_width :]
    return (
        layer_output,
        input_gradient,
        sums_by_row[0],
        sums_by_row[1],
        projection_gradient,
        query_value_gradient,
        output_gradient,
        sums_by_row[2],
        sums_by_row[3],
        sums_by_row[4],
        expand_gradient,
        expand_bias_gradient,
        contract_gradient,
        sums_by_row[5],
    )


def solution(mesh):
    placed = (
        P(("dp", "tensor"), None),
        P(),
        P(),
        P(),
        P(None, None, "tensor"),
        P(None, "tensor"),
        P("tensor", None),
        P(),
        P(),
        P(),
        P(None, "tensor"),
        P("tensor"),
        P("tensor", None),
        P(),
        P(("dp", "tensor"), None),
    )
    return jax.shard_map(
        shards,
        mesh=mesh,
        in_specs=placed,
        out_specs=(
            P(("dp", "tensor"), None),
            P(("dp", "tensor"), None),
            P("tensor"),
            P("tensor"),
            P(None, None, "tensor"),
            P(None, "tensor"),
            P("tensor", None),
            P("tensor"),
            P("tensor"),
            P("tensor"),
            P(None, "tensor"),
            P("tensor"),
            P("tensor", None),
            P("tensor"),
        ),
        check_vma=False,
    )
```

```python
import functools
import math

import jax
import jax.numpy as jnp
from jax import lax
from jax.experimental import pallas as pl
from jax.experimental.pallas import tpu as pltpu
from jax.sharding import PartitionSpec as P

HEAD_DIM = 128
BLOCK = 512
EPSILON = 1e-05
SCALE = HEAD_DIM ** (-0.5)
SCALE_LOG2 = SCALE * math.log2(math.e)
MASKED = -1e30
VMEM_LIMIT = 48 * 1024 * 1024


def dot(a, b, contract):
    return lax.dot_general(a, b, (contract, ((), ())), preferred_element_type=jnp.float32)


def segment_start(position, first, second):
    return jnp.where(position >= second, second, jnp.where(position >= first, first, 0))


def segment_end(position, first, second, rows):
    return jnp.where(position >= second, rows, jnp.where(position >= first, second, first))


def attend_kernel(block, bounds_ref, q_ref, k_ref, v_ref, out_ref, total_ref):
    query_block = pl.program_id(1)
    first, second = bounds_ref[0], bounds_ref[1]
    offset = query_block * block
    q = q_ref[...]
    q_pos = offset + lax.broadcasted_iota(jnp.int32, (1, block), 1)
    start = segment_start(q_pos, first, second)
    k_row = lax.broadcasted_iota(jnp.int32, (block, block), 0)

    def step(key_block, carry):
        highest, row_sum, acc = carry
        rows = pl.ds(pl.multiple_of(key_block * block, block), block)
        scores = dot(k_ref[rows, :], q, ((1,), (1,)))
        base = key_block * block
        allowed = (k_row <= q_pos - base) & (k_row >= start - base)
        scores = jnp.where(allowed, scores * SCALE_LOG2, MASKED)
        new_highest = jnp.maximum(highest, jnp.max(scores, axis=0, keepdims=True))
        weights = jnp.exp2(scores - new_highest)
        decay = jnp.exp2(highest - new_highest)
        row_sum = row_sum * decay + jnp.sum(weights, axis=0, keepdims=True)
        acc = acc * decay + dot(v_ref[rows, :], weights.astype(jnp.bfloat16), ((0,), (0,)))
        return new_highest, row_sum, acc

    low = segment_start(offset, first, second) // block
    highest, row_sum, acc = lax.fori_loop(
        low,
        query_block + 1,
        step,
        (
            jnp.full((1, block), MASKED, jnp.float32),
            jnp.zeros((1, block), jnp.float32),
            jnp.zeros((HEAD_DIM, block), jnp.float32),
        ),
    )
    out_ref[...] = jnp.transpose(acc / row_sum).astype(jnp.bfloat16)
    total_ref[0] = highest + jnp.log2(row_sum)


def attend(bounds, projected, local_heads):
    rows = projected.shape[0]
    block = min(BLOCK, rows)
    return pl.pallas_call(
        functools.partial(attend_kernel, block),
        grid_spec=pltpu.PrefetchScalarGridSpec(
            num_scalar_prefetch=1,
            grid=(local_heads, rows // block),
            in_specs=[
                pl.BlockSpec((block, HEAD_DIM), lambda h, i, _: (i, h)),
                pl.BlockSpec((rows, HEAD_DIM), lambda h, i, _: (0, local_heads + h)),
                pl.BlockSpec((rows, HEAD_DIM), lambda h, i, _: (0, 2 * local_heads + h)),
            ],
            out_specs=[
                pl.BlockSpec((block, HEAD_DIM), lambda h, i, _: (i, h)),
                pl.BlockSpec((1, 1, block), lambda h, i, _: (h, 0, i)),
            ],
        ),
        out_shape=[
            jax.ShapeDtypeStruct((rows, local_heads * HEAD_DIM), jnp.bfloat16),
            jax.ShapeDtypeStruct((local_heads, 1, rows), jnp.float32),
        ],
        compiler_params=pltpu.CompilerParams(vmem_limit_bytes=VMEM_LIMIT),
        cost_estimate=pl.CostEstimate(
            flops=4 * local_heads * rows * rows * HEAD_DIM,
            bytes_accessed=8 * rows * local_heads * HEAD_DIM,
            transcendentals=local_heads * rows * rows,
        ),
    )(bounds, projected, projected, projected)


def attend_back_kernel(
    block,
    local_heads,
    bounds_ref,
    q_ref,
    k_ref,
    v_ref,
    grad_ref,
    context_ref,
    total_ref,
    out_ref,
    query_acc,
    key_acc,
    value_acc,
    inner_ref,
):
    head = pl.program_id(0)
    first, second = bounds_ref[0], bounds_ref[1]
    rows = q_ref.shape[0]
    width = local_heads * HEAD_DIM
    k_row = lax.broadcasted_iota(jnp.int32, (block, block), 0)
    q_col = lax.broadcasted_iota(jnp.int32, (1, block), 1)
    for i in range(rows // block):
        part = pl.ds(i * block, block)
        product = grad_ref[part, :].astype(jnp.float32) * context_ref[part, :].astype(jnp.float32)
        inner_ref[:, part] = jnp.sum(jnp.transpose(product), axis=0, keepdims=True)
    query_acc[...] = jnp.zeros_like(query_acc)

    def key_step(key_block, _):
        base = pl.multiple_of(key_block * block, block)
        key_rows = pl.ds(base, block)
        key_acc[...] = jnp.zeros_like(key_acc)
        value_acc[...] = jnp.zeros_like(value_acc)

        def query_step(query_block, _):
            offset = pl.multiple_of(query_block * block, block)
            query_rows = pl.ds(offset, block)
            k = k_ref[key_rows, :]
            q = q_ref[query_rows, :]
            grad = grad_ref[query_rows, :]
            q_pos = offset + q_col
            start = segment_start(q_pos, first, second)
            scores = dot(k, q, ((1,), (1,)))
            allowed = (k_row <= q_pos - base) & (k_row >= start - base)
            exponent = jnp.where(
                allowed, scores * SCALE_LOG2 - total_ref[0, :, query_rows], MASKED
            )
            weights = jnp.exp2(exponent)
            grad_weights = dot(v_ref[key_rows, :], grad, ((1,), (1,)))
            score_grad = (weights * (grad_weights - inner_ref[:, query_rows])).astype(jnp.bfloat16)
            value_acc[...] += dot(weights.astype(jnp.bfloat16), grad, ((1,), (0,)))
            key_acc[...] += dot(score_grad, q, ((1,), (0,)))
            query_acc[query_rows, :] += dot(score_grad, k, ((0,), (0,)))
            return 0

        last = segment_end(base + block - 1, first, second, rows) - 1
        lax.fori_loop(key_block, last // block + 1, query_step, 0)
        key_columns = pl.ds(pl.multiple_of(width + head * HEAD_DIM, HEAD_DIM), HEAD_DIM)
        value_columns = pl.ds(pl.multiple_of(2 * width + head * HEAD_DIM, HEAD_DIM), HEAD_DIM)
        out_ref[key_rows, key_columns] = (key_acc[...] * SCALE).astype(jnp.bfloat16)
        out_ref[key_rows, value_columns] = value_acc[...].astype(jnp.bfloat16)
        return 0

    lax.fori_loop(0, rows // block, key_step, 0)
    query_columns = pl.ds(pl.multiple_of(head * HEAD_DIM, HEAD_DIM), HEAD_DIM)
    out_ref[:, query_columns] = (query_acc[...] * SCALE).astype(jnp.bfloat16)


def attend_back(bounds, projected, grad_context, context, totals, local_heads):
    rows = projected.shape[0]
    block = min(BLOCK, rows)
    width = local_heads * HEAD_DIM
    column = pl.BlockSpec((rows, HEAD_DIM), lambda h, _: (0, h))
    return pl.pallas_call(
        functools.partial(attend_back_kernel, block, local_heads),
        grid_spec=pltpu.PrefetchScalarGridSpec(
            num_scalar_prefetch=1,
            grid=(local_heads,),
            in_specs=[
                column,
                pl.BlockSpec((rows, HEAD_DIM), lambda h, _: (0, local_heads + h)),
                pl.BlockSpec((rows, HEAD_DIM), lambda h, _: (0, 2 * local_heads + h)),
                column,
                column,
                pl.BlockSpec((1, 1, rows), lambda h, _: (h, 0, 0)),
            ],
            out_specs=pl.BlockSpec((rows, 3 * width), lambda h, _: (0, 0)),
            scratch_shapes=[
                pltpu.VMEM((rows, HEAD_DIM), jnp.float32),
                pltpu.VMEM((block, HEAD_DIM), jnp.float32),
                pltpu.VMEM((block, HEAD_DIM), jnp.float32),
                pltpu.VMEM((1, rows), jnp.float32),
            ],
        ),
        out_shape=jax.ShapeDtypeStruct((rows, 3 * width), jnp.bfloat16),
        compiler_params=pltpu.CompilerParams(vmem_limit_bytes=VMEM_LIMIT),
        cost_estimate=pl.CostEstimate(
            flops=10 * local_heads * rows * rows * HEAD_DIM,
            bytes_accessed=16 * rows * width,
            transcendentals=local_heads * rows * rows,
        ),
    )(bounds, projected, projected, projected, grad_context, context, totals)


def normalize(values):
    center = values - jnp.mean(values, axis=-1, keepdims=True)
    inverse = lax.rsqrt(jnp.mean(center * center, axis=-1, keepdims=True) + EPSILON)
    return center * inverse, inverse


def normalize_back(grad, gain, unit, inverse):
    scaled = grad * gain
    return inverse * (
        scaled
        - jnp.mean(scaled, axis=-1, keepdims=True)
        - unit * jnp.mean(scaled * unit, axis=-1, keepdims=True)
    )


def gelu_tanh(values):
    return jax.nn.gelu(values, approximate=True)


def after(value, *earlier):
    return lax.optimization_barrier((value,) + earlier)[0]


def ring_order(chips):
    return [c for c in range(chips) if c == 0 or c % 2] + [
        c for c in reversed(range(2, chips)) if c % 2 == 0
    ]


def ring_step(value):
    size = lax.axis_size("tensor")
    order = ring_order(size // 2)
    pairs = []
    for place, chip in enumerate(order):
        following = order[(place + 1) % len(order)]
        pairs += [(2 * chip, 2 * following), (2 * chip + 1, 2 * following + 1)]
    return lax.ppermute(value, "tensor", pairs)


def swap_cores(value):
    return lax.ppermute(value, "tensor", [(i, i ^ 1) for i in range(lax.axis_size("tensor"))])


def ring_chip(step):
    chips = lax.axis_size("tensor") // 2
    order = ring_order(chips)
    places = jnp.array([order.index(c) for c in range(chips)], jnp.int32)
    place = places[lax.axis_index("tensor") // 2]
    return jnp.array(order, jnp.int32)[(place + chips - step) % chips]


def ring_gather(block):
    moving = block
    pairs = []
    for step in range(lax.axis_size("tensor") // 2):
        if step:
            moving = ring_step(moving)
        pairs.append((moving, swap_cores(moving)))
    return pairs


def ring_scatter(part, ties=()):
    arrivals = []
    chips = lax.axis_size("tensor") // 2
    for step in list(range(1, chips)) + [0]:
        mine, other = part(step)
        total = mine.astype(jnp.float32) + swap_cores(other).astype(jnp.float32)
        if arrivals:
            total = total + arrivals[-1].astype(jnp.float32)
        if step:
            arrived = ring_step(total.astype(jnp.bfloat16))
            if len(arrivals) < len(ties):
                arrived = after(arrived, *ties[len(arrivals)])
            arrivals.append(arrived)
    return total, arrivals


def in_order(pairs):
    size = lax.axis_size("tensor")
    core = lax.axis_index("tensor") % 2
    block = pairs[0][0]
    full = jnp.zeros((size,) + block.shape, block.dtype)
    for step, (mine, other) in enumerate(pairs):
        chip = ring_chip(step)
        full = lax.dynamic_update_index_in_dim(full, mine, 2 * chip + core, 0)
        full = lax.dynamic_update_index_in_dim(full, other, 2 * chip + 1 - core, 0)
    return full


def flip_dp(value, bit):
    size = lax.axis_size("dp")
    return lax.ppermute(value, "dp", [(i, i ^ bit) for i in range(size)])


def dp_bits():
    return [1 << i for i in range((lax.axis_size("dp") - 1).bit_length())]


def sum_job(value, bits, axis=0):
    me = lax.axis_index("dp")
    for bit in bits:
        half = value.shape[axis] // 2
        up = (me & bit) != 0
        keep = lax.dynamic_slice_in_dim(value, jnp.where(up, half, 0), half, axis)
        give = lax.dynamic_slice_in_dim(value, jnp.where(up, 0, half), half, axis)
        (got,) = yield [(give, bit)]
        value = (keep.astype(jnp.float32) + got.astype(jnp.float32)).astype(value.dtype)
    blocks = [(0, value)]
    wave = [(0, value, bits[::-1])]
    while wave:
        sends = [
            (mask ^ bit, block, bit, left[place + 1 :])
            for mask, block, left in wave
            for place, bit in enumerate(left)
        ]
        if not sends:
            break
        got = yield [(block, bit) for _, block, bit, _ in sends]
        wave = [(mask, block, left) for (mask, _, _, left), block in zip(sends, got)]
        blocks += [(mask, block) for mask, block, _ in wave]
    return blocks


class Exchange:
    def __init__(self):
        self.jobs = {}
        self.done = {}
        self.flying = {}

    def add(self, name, job):
        self.jobs[name] = job
        self._advance(name, None)

    def _advance(self, name, got):
        try:
            sends = self.jobs[name].send(got)
        except StopIteration as stop:
            self.done[name] = stop.value
            del self.jobs[name]
            return
        with jax.named_scope("dp_" + name):
            self.flying[name] = [flip_dp(value, bit) for value, bit in sends]

    def hop(self, *ties):
        names = list(self.flying)
        flat = [value for name in names for value in self.flying[name]]
        flat = lax.optimization_barrier(tuple(flat) + ties)
        place = 0
        for name in names:
            count = len(self.flying.pop(name))
            self._advance(name, list(flat[place : place + count]))
            place += count
        return flat[place:] if len(ties) != 1 else flat[-1]


def dp_blocks(value, bits, ties):
    blocks = [(0, value, 0)]
    for bit in bits:
        for mask, block, hops in list(blocks):
            got = flip_dp(block, bit)
            if hops < len(ties):
                got = after(got, *ties[hops])
            blocks.append((mask ^ bit, got, hops + 1))
    return [(mask, block) for mask, block, _ in blocks]


def cut_place(mask, bits, size):
    device = lax.axis_index("dp") ^ mask
    place = 0
    for bit in bits:
        size //= 2
        place = place + jnp.where((device & bit) != 0, size, 0)
    return place


def put(full, block, row, column=0):
    return lax.dynamic_update_slice(full, block.astype(full.dtype), (row, column))


def small_sum(value, axes):
    for axis in axes:
        size = lax.axis_size(axis)
        bit = 1
        while bit < size:
            value = value + lax.ppermute(value, axis, [(i, i ^ bit) for i in range(size)])
            bit *= 2
    return value


def shards(
    tokens,
    lengths,
    attention_gain,
    attention_shift,
    query_key_value,
    query_value_bias,
    output_weight,
    output_bias,
    feedforward_gain,
    feedforward_shift,
    expand_weight,
    expand_bias,
    contract_weight,
    contract_bias,
    cotangent,
):
    bf16, f32 = jnp.bfloat16, jnp.float32
    shard_rows, features = tokens.shape
    tensor_size = lax.axis_size("tensor")
    group_count = lax.axis_size("dp")
    group = lax.axis_index("dp")
    rank = lax.axis_index("tensor")
    core = rank % 2
    chips = tensor_size // 2
    group_rows = shard_rows * tensor_size
    local_width = query_key_value.shape[2]
    local_heads = local_width // HEAD_DIM
    bounds = jnp.cumsum(lengths, axis=1)
    own_bounds = lax.dynamic_index_in_dim(bounds, group, 0, keepdims=False)
    own_count = own_bounds[-1]
    share = own_count.astype(f32) / jnp.sum(bounds[:, -1]).astype(f32)
    local_rows = rank * shard_rows + jnp.arange(shard_rows, dtype=jnp.int32)
    local_live = (local_rows < own_count).astype(f32)[:, None]

    def dot(a, b, a_axis, b_axis):
        return lax.dot_general(
            a, b, (((a_axis,), (b_axis,)), ((), ())), preferred_element_type=jnp.float32
        )

    def chip_rows(rows, step):
        first = ring_chip(step) * 2 * shard_rows
        return jnp.concatenate(
            [
                lax.dynamic_slice_in_dim(rows, first + core * shard_rows, shard_rows),
                lax.dynamic_slice_in_dim(rows, first + (1 - core) * shard_rows, shard_rows),
            ],
            axis=0,
        )

    def ordered(blocks):
        return in_order([(b[:shard_rows], b[shard_rows:]) for b in blocks]).reshape(
            group_rows, blocks[0].shape[1]
        )

    input_rows = tokens.astype(f32)
    unit_one, inverse_one = normalize(input_rows)
    normed_rows = (unit_one * attention_gain + attention_shift).astype(bf16)
    normed = lax.all_gather(normed_rows, "tensor", axis=0, tiled=True)

    columns = features // group_count
    moving = lax.dynamic_slice_in_dim(output_weight, group * columns, columns, 1)
    pieces = [moving]
    for _ in range(1, chips):
        with jax.named_scope("weight_ring"):
            moving = ring_step(moving)
        pieces.append(moving)
    bits = dp_bits()
    pieces = jnp.concatenate(pieces, axis=0)
    half = pieces.shape[0] // 2

    weight_own = jnp.zeros((2 * half, features), bf16)
    with jax.named_scope("weight_dp"):
        for start, order in ((0, bits), (half, bits[::-1])):
            for mask, block in dp_blocks(pieces[start : start + half], order, []):
                weight_own = put(weight_own, block, start, (group ^ mask) * columns)
    weight_other = swap_cores(weight_own)

    weight_flat = query_key_value.reshape(features, 3 * local_width)
    bias_flat = jnp.concatenate(
        [query_value_bias[0], jnp.zeros_like(query_value_bias[0]), query_value_bias[1]]
    )
    normed, weight_own, weight_other, weight_flat = lax.optimization_barrier(
        (normed, weight_own, weight_other, weight_flat)
    )
    grad_rows_low = jnp.where(local_live > 0, cotangent, jnp.zeros_like(cotangent))
    grad_out = lax.all_gather(after(grad_rows_low, normed), "tensor", axis=0, tiled=True)

    projected = (dot(normed, weight_flat, 1, 0) + bias_flat).astype(bf16)
    context, totals = attend(own_bounds, projected, local_heads)

    arrived = lax.all_to_all(
        context.reshape(tensor_size, shard_rows, local_width), "tensor", 0, 0, tiled=True
    )

    def heads_of(parity):
        return jnp.concatenate(
            [
                lax.dynamic_index_in_dim(arrived, 2 * ring_chip(step) + parity, 0, False)
                for step in range(chips)
            ],
            axis=1,
        )

    context_own, context_other = heads_of(core), heads_of(1 - core)
    hidden = (
        input_rows
        + dot(context_own, weight_own, 1, 0)
        + dot(context_other, weight_other, 1, 0)
        + output_bias
    )
    unit_two, inverse_two = normalize(hidden)
    mixed_rows = (unit_two * feedforward_gain + feedforward_shift).astype(bf16)

    mixed, activated, grad_pre, mixed_terms, mixed_arrivals = [], [], [], [], []
    mixed_sent = []
    moving = after(mixed_rows, grad_out)

    def mixed_step(step):
        mixed.append(jnp.concatenate([moving, swap_cores(moving)], axis=0))
        rows = mixed[step]
        if step > 2:
            rows = after(rows, mixed_sent[step - 2])
        grad_activated = dot(chip_rows(grad_out, step), contract_weight, 1, 1)
        pre_act = dot(rows, expand_weight, 1, 0) + expand_bias
        value, gelu_pull = jax.vjp(gelu_tanh, pre_act)
        activated.append(value.astype(bf16))
        grad_pre.append(gelu_pull(grad_activated)[0].astype(bf16))
        mixed_terms.append(dot(grad_pre[step], expand_weight, 1, 1).astype(bf16))

    def chip_total(terms, arrivals):
        total = terms[:shard_rows].astype(f32) + swap_cores(terms[shard_rows:]).astype(f32)
        return total + arrivals[-1].astype(f32) if arrivals else total

    for step in range(chips):
        with jax.named_scope(f"mixed_ring{step}"):
            if step:
                moving = ring_step(moving if step < 3 else after(moving, mixed_terms[step - 2]))
            mixed_step(step)
        if step:
            with jax.named_scope(f"grad_mixed_ring{step}"):
                total = chip_total(mixed_terms[step], mixed_arrivals)
                mixed_sent.append(total.astype(bf16))
                mixed_arrivals.append(ring_step(mixed_sent[-1]))
    second = mixed_arrivals[-2]
    activated_all = after(ordered(activated), second)
    grad_pre_all = after(ordered(grad_pre), second)
    mixed_all = ordered(mixed)
    with jax.named_scope("contract_gradient"):
        contract_local = (share * dot(activated_all, grad_out, 0, 0)).astype(bf16)
    with jax.named_scope("expand_gradient"):
        expand_local = (share * dot(mixed_all, grad_pre_all, 0, 0)).astype(bf16)
    mixed_arrivals[-1] = after(mixed_arrivals[-1], contract_local, expand_local)
    with jax.named_scope("grad_mixed_own"):
        grad_mixed = chip_total(mixed_terms[0], mixed_arrivals)

    grad_local = grad_rows_low.astype(f32)
    grad_hidden = grad_local + normalize_back(grad_mixed, feedforward_gain, unit_two, inverse_two)
    grad_hidden_low = grad_hidden.astype(bf16)
    with jax.named_scope("grad_hidden_gather"):
        grad_hidden_all = lax.all_gather(grad_hidden_low, "tensor", axis=0, tiled=True)

    exchange = Exchange()
    exchange.add("contract", sum_job(contract_local, bits))
    exchange.add("expand", sum_job(expand_local, bits[::-1]))
    branch_terms = [
        dot(after(block, grad_hidden_low), contract_weight, 1, 0).astype(bf16) for block in activated
    ]
    branch_totals = [
        block[:shard_rows].astype(f32) + swap_cores(block[shard_rows:]).astype(f32)
        for block in branch_terms
    ]
    branch_sent = branch_totals[1].astype(bf16)
    for _ in bits:
        grad_hidden_low = exchange.hop(grad_hidden_low, *branch_terms, branch_sent)[0]
    grad_hidden_all, branch_sent = lax.optimization_barrier(
        (after(grad_hidden_all, grad_hidden_low), branch_sent)
    )
    with jax.named_scope("branch_ring1"):
        branch_arrived = ring_step(branch_sent)
    with jax.named_scope("grad_context"):
        grad_context = dot(grad_hidden_all, output_weight, 1, 1).astype(bf16)

    def branch_step(step):
        with jax.named_scope(f"branch_ring{step}"):
            total = branch_totals[step] + branch_arrived.astype(f32)
            return ring_step(total.astype(bf16))

    projected_grad = attend_back(own_bounds, projected, grad_context, context, totals, local_heads)
    projected_grad, branch_arrived = lax.optimization_barrier((projected_grad, branch_arrived))
    branch_arrived = branch_step(2)
    with jax.named_scope("normed_terms"):
        normed_terms = dot(projected_grad, weight_flat, 1, 1).astype(bf16)
    normed_terms, branch_arrived = exchange.hop(normed_terms, branch_arrived)
    projected_late = after(projected_grad, normed_terms)
    with jax.named_scope("grad_normed_scatter"):
        grad_normed = lax.psum_scatter(
            normed_terms, "tensor", scatter_dimension=0, tiled=True
        ).astype(f32)

    with jax.named_scope("projection_gradient"):
        projection_local = (share * dot(normed, projected_late, 0, 0)).astype(bf16)
    with jax.named_scope("output_gradient"):
        output_local = (share * dot(context, after(grad_hidden_all, normed_terms), 0, 0)).astype(
            bf16
        )
    cut = projection_local.shape[0] // 2
    projection_orders = ((0, bits), (cut, bits[::-1]))
    for start, order in projection_orders:
        exchange.add(f"projection{start}", sum_job(projection_local[start : start + cut], order))
    exchange.add("output", sum_job(output_local, bits))
    sums_by_row = share * jnp.stack(
        [
            jnp.sum(grad_normed * unit_one, axis=0),
            jnp.sum(grad_normed, axis=0),
            jnp.sum(grad_hidden, axis=0),
            jnp.sum(grad_mixed * unit_two, axis=0),
            jnp.sum(grad_mixed, axis=0),
            jnp.sum(grad_local, axis=0),
        ]
    )
    column_sums = jnp.sum(projected_grad.astype(f32), axis=0)
    sums_by_width = share * jnp.concatenate(
        [
            column_sums[:local_width],
            column_sums[2 * local_width :],
            jnp.sum(grad_pre_all.astype(f32), axis=0),
        ]
    )
    own_columns = features // tensor_size
    for _ in bits[1:]:
        exchange.hop()
    branch_arrived = exchange.hop(branch_arrived)
    sums_by_row, branch_arrived = exchange.hop(sums_by_row, branch_arrived)
    for step in range(3, chips):
        branch_arrived = branch_step(step)
    while exchange.flying:
        exchange.hop()
    with jax.named_scope("small_sums"):
        sums = small_sum(jnp.concatenate([sums_by_row.reshape(-1), sums_by_width]), ("dp",))
        sums, branch_arrived = lax.optimization_barrier((sums, branch_arrived))
        sums_by_width = sums[sums_by_row.size :]
        sums_by_row = small_sum(
            sums[: sums_by_row.size].reshape(sums_by_row.shape), ("tensor",)
        )
        sums_by_row = lax.dynamic_slice_in_dim(sums_by_row, rank * own_columns, own_columns, 1)
    projection_parts = [
        (start, order, exchange.done[f"projection{start}"]) for start, order in projection_orders
    ]
    zero = after(jnp.zeros((), f32), normed_terms)
    input_gradient = (
        grad_hidden + normalize_back(grad_normed, attention_gain, unit_one, inverse_one)
    ).astype(bf16)

    contract_gradient = jnp.broadcast_to(zero, contract_local.shape)
    for mask, block in exchange.done["contract"]:
        contract_gradient = put(
            contract_gradient, block, cut_place(mask, bits, contract_local.shape[0])
        )
    expand_gradient = jnp.broadcast_to(zero, expand_local.shape)
    for mask, block in exchange.done["expand"]:
        expand_gradient = put(
            expand_gradient, block, cut_place(mask, bits[::-1], expand_local.shape[0])
        )
    projection_gradient = jnp.broadcast_to(zero.astype(bf16), projection_local.shape)
    for start, order, blocks in projection_parts:
        for mask, block in blocks:
            projection_gradient = put(
                projection_gradient, block, start + cut_place(mask, order, cut)
            )
    projection_gradient = projection_gradient.reshape(features, 3, local_width).astype(f32)
    output_gradient = jnp.broadcast_to(zero, output_local.shape)
    for mask, block in exchange.done["output"]:
        output_gradient = put(
            output_gradient, block, cut_place(mask, bits, output_local.shape[0])
        )

    branch = branch_totals[0] + branch_arrived.astype(f32)
    layer_output = (local_live * (hidden + branch + contract_bias)).astype(bf16)
    query_value_gradient = sums_by_width[: 2 * local_width].reshape(2, local_width)
    expand_bias_gradient = sums_by_width[2 * local_width :]
    return (
        layer_output,
        input_gradient,
        sums_by_row[0],
        sums_by_row[1],
        projection_gradient,
        query_value_gradient,
        output_gradient,
        sums_by_row[2],
        sums_by_row[3],
        sums_by_row[4],
        expand_gradient,
        expand_bias_gradient,
        contract_gradient,
        sums_by_row[5],
    )


def solution(mesh):
    placed = (
        P(("dp", "tensor"), None),
        P(),
        P(),
        P(),
        P(None, None, "tensor"),
        P(None, "tensor"),
        P("tensor", None),
        P(),
        P(),
        P(),
        P(None, "tensor"),
        P("tensor"),
        P("tensor", None),
        P(),
        P(("dp", "tensor"), None),
    )
    return jax.shard_map(
        shards,
        mesh=mesh,
        in_specs=placed,
        out_specs=(
            P(("dp", "tensor"), None),
            P(("dp", "tensor"), None),
            P("tensor"),
            P("tensor"),
            P(None, None, "tensor"),
            P(None, "tensor"),
            P("tensor", None),
            P("tensor"),
            P("tensor"),
            P("tensor"),
            P(None, "tensor"),
            P("tensor"),
            P("tensor", None),
            P("tensor"),
        ),
        check_vma=False,
    )
```

```python
import functools
import math

import jax
import jax.numpy as jnp
from jax import lax
from jax.experimental import pallas as pl
from jax.experimental.pallas import tpu as pltpu
from jax.sharding import PartitionSpec as P

HEAD_DIM = 128
BLOCK = 512
EPSILON = 1e-05
SCALE = HEAD_DIM ** (-0.5)
SCALE_LOG2 = SCALE * math.log2(math.e)
MASKED = -1e30
VMEM_LIMIT = 48 * 1024 * 1024


def dot(a, b, contract):
    return lax.dot_general(a, b, (contract, ((), ())), preferred_element_type=jnp.float32)


def segment_start(position, first, second):
    return jnp.where(position >= second, second, jnp.where(position >= first, first, 0))


def segment_end(position, first, second, rows):
    return jnp.where(position >= second, rows, jnp.where(position >= first, second, first))


def attend_kernel(block, bounds_ref, q_ref, k_ref, v_ref, out_ref, total_ref):
    query_block = pl.program_id(1)
    first, second = bounds_ref[0], bounds_ref[1]
    offset = query_block * block
    q = q_ref[...]
    q_pos = offset + lax.broadcasted_iota(jnp.int32, (1, block), 1)
    start = segment_start(q_pos, first, second)
    k_row = lax.broadcasted_iota(jnp.int32, (block, block), 0)

    def step(key_block, carry):
        highest, row_sum, acc = carry
        rows = pl.ds(pl.multiple_of(key_block * block, block), block)
        scores = dot(k_ref[rows, :], q, ((1,), (1,)))
        base = key_block * block
        allowed = (k_row <= q_pos - base) & (k_row >= start - base)
        scores = jnp.where(allowed, scores * SCALE_LOG2, MASKED)
        new_highest = jnp.maximum(highest, jnp.max(scores, axis=0, keepdims=True))
        weights = jnp.exp2(scores - new_highest)
        decay = jnp.exp2(highest - new_highest)
        row_sum = row_sum * decay + jnp.sum(weights, axis=0, keepdims=True)
        acc = acc * decay + dot(v_ref[rows, :], weights.astype(jnp.bfloat16), ((0,), (0,)))
        return new_highest, row_sum, acc

    low = segment_start(offset, first, second) // block
    highest, row_sum, acc = lax.fori_loop(
        low,
        query_block + 1,
        step,
        (
            jnp.full((1, block), MASKED, jnp.float32),
            jnp.zeros((1, block), jnp.float32),
            jnp.zeros((HEAD_DIM, block), jnp.float32),
        ),
    )
    out_ref[...] = jnp.transpose(acc / row_sum).astype(jnp.bfloat16)
    total_ref[0] = highest + jnp.log2(row_sum)


def attend(bounds, projected, local_heads):
    rows = projected.shape[0]
    block = min(BLOCK, rows)
    return pl.pallas_call(
        functools.partial(attend_kernel, block),
        grid_spec=pltpu.PrefetchScalarGridSpec(
            num_scalar_prefetch=1,
            grid=(local_heads, rows // block),
            in_specs=[
                pl.BlockSpec((block, HEAD_DIM), lambda h, i, _: (i, h)),
                pl.BlockSpec((rows, HEAD_DIM), lambda h, i, _: (0, local_heads + h)),
                pl.BlockSpec((rows, HEAD_DIM), lambda h, i, _: (0, 2 * local_heads + h)),
            ],
            out_specs=[
                pl.BlockSpec((block, HEAD_DIM), lambda h, i, _: (i, h)),
                pl.BlockSpec((1, 1, block), lambda h, i, _: (h, 0, i)),
            ],
        ),
        out_shape=[
            jax.ShapeDtypeStruct((rows, local_heads * HEAD_DIM), jnp.bfloat16),
            jax.ShapeDtypeStruct((local_heads, 1, rows), jnp.float32),
        ],
        compiler_params=pltpu.CompilerParams(vmem_limit_bytes=VMEM_LIMIT),
        cost_estimate=pl.CostEstimate(
            flops=4 * local_heads * rows * rows * HEAD_DIM,
            bytes_accessed=8 * rows * local_heads * HEAD_DIM,
            transcendentals=local_heads * rows * rows,
        ),
    )(bounds, projected, projected, projected)


def attend_back_kernel(
    block,
    local_heads,
    bounds_ref,
    q_ref,
    k_ref,
    v_ref,
    grad_ref,
    context_ref,
    total_ref,
    out_ref,
    query_acc,
    key_acc,
    value_acc,
    inner_ref,
):
    head = pl.program_id(0)
    first, second = bounds_ref[0], bounds_ref[1]
    rows = q_ref.shape[0]
    width = local_heads * HEAD_DIM
    k_row = lax.broadcasted_iota(jnp.int32, (block, block), 0)
    q_col = lax.broadcasted_iota(jnp.int32, (1, block), 1)
    for i in range(rows // block):
        part = pl.ds(i * block, block)
        product = grad_ref[part, :].astype(jnp.float32) * context_ref[part, :].astype(jnp.float32)
        inner_ref[:, part] = jnp.sum(jnp.transpose(product), axis=0, keepdims=True)
    query_acc[...] = jnp.zeros_like(query_acc)

    def key_step(key_block, _):
        base = pl.multiple_of(key_block * block, block)
        key_rows = pl.ds(base, block)
        key_acc[...] = jnp.zeros_like(key_acc)
        value_acc[...] = jnp.zeros_like(value_acc)

        def query_step(query_block, _):
            offset = pl.multiple_of(query_block * block, block)
            query_rows = pl.ds(offset, block)
            k = k_ref[key_rows, :]
            q = q_ref[query_rows, :]
            grad = grad_ref[query_rows, :]
            q_pos = offset + q_col
            start = segment_start(q_pos, first, second)
            scores = dot(k, q, ((1,), (1,)))
            allowed = (k_row <= q_pos - base) & (k_row >= start - base)
            exponent = jnp.where(
                allowed, scores * SCALE_LOG2 - total_ref[0, :, query_rows], MASKED
            )
            weights = jnp.exp2(exponent)
            grad_weights = dot(v_ref[key_rows, :], grad, ((1,), (1,)))
            score_grad = (weights * (grad_weights - inner_ref[:, query_rows])).astype(jnp.bfloat16)
            value_acc[...] += dot(weights.astype(jnp.bfloat16), grad, ((1,), (0,)))
            key_acc[...] += dot(score_grad, q, ((1,), (0,)))
            query_acc[query_rows, :] += dot(score_grad, k, ((0,), (0,)))
            return 0

        last = segment_end(base + block - 1, first, second, rows) - 1
        lax.fori_loop(key_block, last // block + 1, query_step, 0)
        key_columns = pl.ds(pl.multiple_of(width + head * HEAD_DIM, HEAD_DIM), HEAD_DIM)
        value_columns = pl.ds(pl.multiple_of(2 * width + head * HEAD_DIM, HEAD_DIM), HEAD_DIM)
        out_ref[key_rows, key_columns] = (key_acc[...] * SCALE).astype(jnp.bfloat16)
        out_ref[key_rows, value_columns] = value_acc[...].astype(jnp.bfloat16)
        return 0

    lax.fori_loop(0, rows // block, key_step, 0)
    query_columns = pl.ds(pl.multiple_of(head * HEAD_DIM, HEAD_DIM), HEAD_DIM)
    out_ref[:, query_columns] = (query_acc[...] * SCALE).astype(jnp.bfloat16)


def attend_back(bounds, projected, grad_context, context, totals, local_heads):
    rows = projected.shape[0]
    block = min(BLOCK, rows)
    width = local_heads * HEAD_DIM
    column = pl.BlockSpec((rows, HEAD_DIM), lambda h, _: (0, h))
    return pl.pallas_call(
        functools.partial(attend_back_kernel, block, local_heads),
        grid_spec=pltpu.PrefetchScalarGridSpec(
            num_scalar_prefetch=1,
            grid=(local_heads,),
            in_specs=[
                column,
                pl.BlockSpec((rows, HEAD_DIM), lambda h, _: (0, local_heads + h)),
                pl.BlockSpec((rows, HEAD_DIM), lambda h, _: (0, 2 * local_heads + h)),
                column,
                column,
                pl.BlockSpec((1, 1, rows), lambda h, _: (h, 0, 0)),
            ],
            out_specs=pl.BlockSpec((rows, 3 * width), lambda h, _: (0, 0)),
            scratch_shapes=[
                pltpu.VMEM((rows, HEAD_DIM), jnp.float32),
                pltpu.VMEM((block, HEAD_DIM), jnp.float32),
                pltpu.VMEM((block, HEAD_DIM), jnp.float32),
                pltpu.VMEM((1, rows), jnp.float32),
            ],
        ),
        out_shape=jax.ShapeDtypeStruct((rows, 3 * width), jnp.bfloat16),
        compiler_params=pltpu.CompilerParams(vmem_limit_bytes=VMEM_LIMIT),
        cost_estimate=pl.CostEstimate(
            flops=10 * local_heads * rows * rows * HEAD_DIM,
            bytes_accessed=16 * rows * width,
            transcendentals=local_heads * rows * rows,
        ),
    )(bounds, projected, projected, projected, grad_context, context, totals)


def normalize(values):
    center = values - jnp.mean(values, axis=-1, keepdims=True)
    inverse = lax.rsqrt(jnp.mean(center * center, axis=-1, keepdims=True) + EPSILON)
    return center * inverse, inverse


def normalize_back(grad, gain, unit, inverse):
    scaled = grad * gain
    return inverse * (
        scaled
        - jnp.mean(scaled, axis=-1, keepdims=True)
        - unit * jnp.mean(scaled * unit, axis=-1, keepdims=True)
    )


def gelu_tanh(values):
    return jax.nn.gelu(values, approximate=True)


def after(value, *earlier):
    return lax.optimization_barrier((value,) + earlier)[0]


def ring_order(chips):
    return [c for c in range(chips) if c == 0 or c % 2] + [
        c for c in reversed(range(2, chips)) if c % 2 == 0
    ]


def ring_step(value):
    size = lax.axis_size("tensor")
    order = ring_order(size // 2)
    pairs = []
    for place, chip in enumerate(order):
        following = order[(place + 1) % len(order)]
        pairs += [(2 * chip, 2 * following), (2 * chip + 1, 2 * following + 1)]
    return lax.ppermute(value, "tensor", pairs)


def swap_cores(value):
    return lax.ppermute(value, "tensor", [(i, i ^ 1) for i in range(lax.axis_size("tensor"))])


def ring_chip(step):
    chips = lax.axis_size("tensor") // 2
    order = ring_order(chips)
    places = jnp.array([order.index(c) for c in range(chips)], jnp.int32)
    place = places[lax.axis_index("tensor") // 2]
    return jnp.array(order, jnp.int32)[(place + chips - step) % chips]


def ring_gather(block):
    moving = block
    pairs = []
    for step in range(lax.axis_size("tensor") // 2):
        if step:
            moving = ring_step(moving)
        pairs.append((moving, swap_cores(moving)))
    return pairs


def ring_scatter(part, ties=()):
    arrivals = []
    chips = lax.axis_size("tensor") // 2
    for step in list(range(1, chips)) + [0]:
        mine, other = part(step)
        total = mine.astype(jnp.float32) + swap_cores(other).astype(jnp.float32)
        if arrivals:
            total = total + arrivals[-1].astype(jnp.float32)
        if step:
            arrived = ring_step(total.astype(jnp.bfloat16))
            if len(arrivals) < len(ties):
                arrived = after(arrived, *ties[len(arrivals)])
            arrivals.append(arrived)
    return total, arrivals


def in_order(pairs):
    size = lax.axis_size("tensor")
    core = lax.axis_index("tensor") % 2
    block = pairs[0][0]
    full = jnp.zeros((size,) + block.shape, block.dtype)
    for step, (mine, other) in enumerate(pairs):
        chip = ring_chip(step)
        full = lax.dynamic_update_index_in_dim(full, mine, 2 * chip + core, 0)
        full = lax.dynamic_update_index_in_dim(full, other, 2 * chip + 1 - core, 0)
    return full


def flip_dp(value, bit):
    size = lax.axis_size("dp")
    return lax.ppermute(value, "dp", [(i, i ^ bit) for i in range(size)])


def dp_bits():
    return [1 << i for i in range((lax.axis_size("dp") - 1).bit_length())]


def sum_job(value, bits, axis=0):
    me = lax.axis_index("dp")
    for bit in bits:
        half = value.shape[axis] // 2
        up = (me & bit) != 0
        keep = lax.dynamic_slice_in_dim(value, jnp.where(up, half, 0), half, axis)
        give = lax.dynamic_slice_in_dim(value, jnp.where(up, 0, half), half, axis)
        (got,) = yield [(give, bit)]
        value = (keep.astype(jnp.float32) + got.astype(jnp.float32)).astype(value.dtype)
    blocks = [(0, value)]
    wave = [(0, value, bits[::-1])]
    while wave:
        sends = [
            (mask ^ bit, block, bit, left[place + 1 :])
            for mask, block, left in wave
            for place, bit in enumerate(left)
        ]
        if not sends:
            break
        got = yield [(block, bit) for _, block, bit, _ in sends]
        wave = [(mask, block, left) for (mask, _, _, left), block in zip(sends, got)]
        blocks += [(mask, block) for mask, block, _ in wave]
    return blocks


class Exchange:
    def __init__(self):
        self.jobs = {}
        self.done = {}
        self.flying = {}

    def add(self, name, job):
        self.jobs[name] = job
        self._advance(name, None)

    def _advance(self, name, got):
        try:
            sends = self.jobs[name].send(got)
        except StopIteration as stop:
            self.done[name] = stop.value
            del self.jobs[name]
            return
        with jax.named_scope("dp_" + name):
            self.flying[name] = [flip_dp(value, bit) for value, bit in sends]

    def hop(self, *ties):
        names = list(self.flying)
        flat = [value for name in names for value in self.flying[name]]
        flat = lax.optimization_barrier(tuple(flat) + ties)
        place = 0
        for name in names:
            count = len(self.flying.pop(name))
            self._advance(name, list(flat[place : place + count]))
            place += count
        return flat[place:] if len(ties) != 1 else flat[-1]


def dp_blocks(value, bits, ties):
    blocks = [(0, value, 0)]
    for bit in bits:
        for mask, block, hops in list(blocks):
            got = flip_dp(block, bit)
            if hops < len(ties):
                got = after(got, *ties[hops])
            blocks.append((mask ^ bit, got, hops + 1))
    return [(mask, block) for mask, block, _ in blocks]


def cut_place(mask, bits, size):
    device = lax.axis_index("dp") ^ mask
    place = 0
    for bit in bits:
        size //= 2
        place = place + jnp.where((device & bit) != 0, size, 0)
    return place


def put(full, block, row, column=0):
    return lax.dynamic_update_slice(full, block.astype(full.dtype), (row, column))


def small_sum(value, axes):
    for axis in axes:
        size = lax.axis_size(axis)
        bit = 1
        while bit < size:
            value = value + lax.ppermute(value, axis, [(i, i ^ bit) for i in range(size)])
            bit *= 2
    return value


def shards(
    tokens,
    lengths,
    attention_gain,
    attention_shift,
    query_key_value,
    query_value_bias,
    output_weight,
    output_bias,
    feedforward_gain,
    feedforward_shift,
    expand_weight,
    expand_bias,
    contract_weight,
    contract_bias,
    cotangent,
):
    bf16, f32 = jnp.bfloat16, jnp.float32
    shard_rows, features = tokens.shape
    tensor_size = lax.axis_size("tensor")
    group_count = lax.axis_size("dp")
    group = lax.axis_index("dp")
    rank = lax.axis_index("tensor")
    core = rank % 2
    chips = tensor_size // 2
    group_rows = shard_rows * tensor_size
    local_width = query_key_value.shape[2]
    local_heads = local_width // HEAD_DIM
    bounds = jnp.cumsum(lengths, axis=1)
    own_bounds = lax.dynamic_index_in_dim(bounds, group, 0, keepdims=False)
    own_count = own_bounds[-1]
    share = own_count.astype(f32) / jnp.sum(bounds[:, -1]).astype(f32)
    local_rows = rank * shard_rows + jnp.arange(shard_rows, dtype=jnp.int32)
    local_live = (local_rows < own_count).astype(f32)[:, None]

    def dot(a, b, a_axis, b_axis):
        return lax.dot_general(
            a, b, (((a_axis,), (b_axis,)), ((), ())), preferred_element_type=jnp.float32
        )

    def chip_rows(rows, step):
        first = ring_chip(step) * 2 * shard_rows
        return jnp.concatenate(
            [
                lax.dynamic_slice_in_dim(rows, first + core * shard_rows, shard_rows),
                lax.dynamic_slice_in_dim(rows, first + (1 - core) * shard_rows, shard_rows),
            ],
            axis=0,
        )

    def ordered(blocks):
        return in_order([(b[:shard_rows], b[shard_rows:]) for b in blocks]).reshape(
            group_rows, blocks[0].shape[1]
        )

    input_rows = tokens.astype(f32)
    unit_one, inverse_one = normalize(input_rows)
    normed_rows = (unit_one * attention_gain + attention_shift).astype(bf16)
    normed = lax.all_gather(normed_rows, "tensor", axis=0, tiled=True)

    columns = features // group_count
    moving = lax.dynamic_slice_in_dim(output_weight, group * columns, columns, 1)
    pieces = [moving]
    for _ in range(1, chips):
        with jax.named_scope("weight_ring"):
            moving = ring_step(moving)
        pieces.append(moving)
    bits = dp_bits()
    pieces = jnp.concatenate(pieces, axis=0)
    half = pieces.shape[0] // 2

    weight_own = jnp.zeros((2 * half, features), bf16)
    with jax.named_scope("weight_dp"):
        for start, order in ((0, bits), (half, bits[::-1])):
            for mask, block in dp_blocks(pieces[start : start + half], order, []):
                weight_own = put(weight_own, block, start, (group ^ mask) * columns)
    weight_other = swap_cores(weight_own)

    weight_flat = query_key_value.reshape(features, 3 * local_width)
    bias_flat = jnp.concatenate(
        [query_value_bias[0], jnp.zeros_like(query_value_bias[0]), query_value_bias[1]]
    )
    normed, weight_own, weight_other, weight_flat = lax.optimization_barrier(
        (normed, weight_own, weight_other, weight_flat)
    )
    grad_rows_low = jnp.where(local_live > 0, cotangent, jnp.zeros_like(cotangent))
    grad_out = lax.all_gather(after(grad_rows_low, normed), "tensor", axis=0, tiled=True)

    projected = (dot(normed, weight_flat, 1, 0) + bias_flat).astype(bf16)
    context, totals = attend(own_bounds, projected, local_heads)

    arrived = lax.all_to_all(
        context.reshape(tensor_size, shard_rows, local_width), "tensor", 0, 0, tiled=True
    )

    def heads_of(parity):
        return jnp.concatenate(
            [
                lax.dynamic_index_in_dim(arrived, 2 * ring_chip(step) + parity, 0, False)
                for step in range(chips)
            ],
            axis=1,
        )

    context_own, context_other = heads_of(core), heads_of(1 - core)
    hidden = (
        input_rows
        + dot(context_own, weight_own, 1, 0)
        + dot(context_other, weight_other, 1, 0)
        + output_bias
    )
    unit_two, inverse_two = normalize(hidden)
    mixed_rows = (unit_two * feedforward_gain + feedforward_shift).astype(bf16)

    mixed, activated, grad_pre, mixed_terms, mixed_arrivals = [], [], [], [], []
    mixed_sent = []
    moving = after(mixed_rows, grad_out)

    def mixed_step(step):
        mixed.append(jnp.concatenate([moving, swap_cores(moving)], axis=0))
        rows = mixed[step]
        if step > 2:
            rows = after(rows, mixed_sent[step - 2])
        grad_activated = dot(chip_rows(grad_out, step), contract_weight, 1, 1)
        pre_act = dot(rows, expand_weight, 1, 0) + expand_bias
        value, gelu_pull = jax.vjp(gelu_tanh, pre_act)
        activated.append(value.astype(bf16))
        grad_pre.append(gelu_pull(grad_activated)[0].astype(bf16))
        mixed_terms.append(dot(grad_pre[step], expand_weight, 1, 1).astype(bf16))

    def chip_total(terms, arrivals):
        total = terms[:shard_rows].astype(f32) + swap_cores(terms[shard_rows:]).astype(f32)
        return total + arrivals[-1].astype(f32) if arrivals else total

    for step in range(chips):
        with jax.named_scope(f"mixed_ring{step}"):
            if step:
                moving = ring_step(moving if step < 3 else after(moving, mixed_terms[step - 2]))
            mixed_step(step)
        if step:
            with jax.named_scope(f"grad_mixed_ring{step}"):
                total = chip_total(mixed_terms[step], mixed_arrivals)
                mixed_sent.append(total.astype(bf16))
                mixed_arrivals.append(ring_step(mixed_sent[-1]))
    second = mixed_arrivals[-2]
    activated_all = after(ordered(activated), second)
    grad_pre_all = after(ordered(grad_pre), second)
    mixed_all = ordered(mixed)
    with jax.named_scope("contract_gradient"):
        contract_local = (share * dot(activated_all, grad_out, 0, 0)).astype(bf16)
    with jax.named_scope("expand_gradient"):
        expand_local = (share * dot(mixed_all, grad_pre_all, 0, 0)).astype(bf16)
    mixed_arrivals[-1] = after(mixed_arrivals[-1], contract_local, expand_local)
    with jax.named_scope("grad_mixed_own"):
        grad_mixed = chip_total(mixed_terms[0], mixed_arrivals)

    grad_local = grad_rows_low.astype(f32)
    grad_hidden = grad_local + normalize_back(grad_mixed, feedforward_gain, unit_two, inverse_two)
    grad_hidden_low = grad_hidden.astype(bf16)
    with jax.named_scope("grad_hidden_gather"):
        grad_hidden_all = lax.all_gather(grad_hidden_low, "tensor", axis=0, tiled=True)

    exchange = Exchange()
    exchange.add("contract", sum_job(contract_local, bits))
    exchange.add("expand", sum_job(expand_local, bits[::-1]))
    branch_terms = [
        dot(after(block, grad_hidden_low), contract_weight, 1, 0).astype(bf16) for block in activated
    ]
    branch_totals = [
        block[:shard_rows].astype(f32) + swap_cores(block[shard_rows:]).astype(f32)
        for block in branch_terms
    ]
    branch_sent = branch_totals[1].astype(bf16)
    for _ in bits:
        grad_hidden_low = exchange.hop(grad_hidden_low, *branch_terms, branch_sent)[0]
    grad_hidden_all, branch_sent = lax.optimization_barrier(
        (after(grad_hidden_all, grad_hidden_low), branch_sent)
    )
    with jax.named_scope("branch_ring1"):
        branch_arrived = ring_step(branch_sent)
    with jax.named_scope("grad_context"):
        grad_context = dot(grad_hidden_all, output_weight, 1, 1).astype(bf16)

    def branch_step(step):
        with jax.named_scope(f"branch_ring{step}"):
            total = branch_totals[step] + branch_arrived.astype(f32)
            return ring_step(total.astype(bf16))

    projected_grad = attend_back(own_bounds, projected, grad_context, context, totals, local_heads)
    projected_grad, branch_arrived = lax.optimization_barrier((projected_grad, branch_arrived))
    branch_arrived = branch_step(2)
    with jax.named_scope("normed_terms"):
        normed_terms = dot(projected_grad, weight_flat, 1, 1).astype(bf16)
    normed_terms, branch_arrived = exchange.hop(normed_terms, branch_arrived)
    projected_late = after(projected_grad, normed_terms)
    with jax.named_scope("grad_normed_scatter"):
        grad_normed = lax.psum_scatter(
            normed_terms, "tensor", scatter_dimension=0, tiled=True
        ).astype(f32)

    with jax.named_scope("projection_gradient"):
        projection_local = (share * dot(normed, projected_late, 0, 0)).astype(bf16)
    with jax.named_scope("output_gradient"):
        output_local = (share * dot(context, after(grad_hidden_all, normed_terms), 0, 0)).astype(
            bf16
        )
    cut = projection_local.shape[0] // 2
    projection_orders = ((0, bits), (cut, bits[::-1]))
    for start, order in projection_orders:
        exchange.add(f"projection{start}", sum_job(projection_local[start : start + cut], order))
    exchange.add("output", sum_job(output_local, bits))
    sums_by_row = share * jnp.stack(
        [
            jnp.sum(grad_normed * unit_one, axis=0),
            jnp.sum(grad_normed, axis=0),
            jnp.sum(grad_hidden, axis=0),
            jnp.sum(grad_mixed * unit_two, axis=0),
            jnp.sum(grad_mixed, axis=0),
            jnp.sum(grad_local, axis=0),
        ]
    )
    column_sums = jnp.sum(projected_grad.astype(f32), axis=0)
    sums_by_width = share * jnp.concatenate(
        [
            column_sums[:local_width],
            column_sums[2 * local_width :],
            jnp.sum(grad_pre_all.astype(f32), axis=0),
        ]
    )
    own_columns = features // tensor_size
    for _ in bits[1:]:
        exchange.hop()
    branch_arrived = exchange.hop(branch_arrived)
    sums_by_row, branch_arrived = exchange.hop(sums_by_row, branch_arrived)
    for step in range(3, chips):
        branch_arrived = branch_step(step)
    while exchange.flying:
        exchange.hop()
    with jax.named_scope("small_sums"):
        sums_by_width = small_sum(sums_by_width, ("dp",))
        sums_by_row = small_sum(sums_by_row, ("dp",))
        sums_by_row, branch_arrived = lax.optimization_barrier((sums_by_row, branch_arrived))
        sums_by_row = small_sum(sums_by_row, ("tensor",))
        sums_by_row = lax.dynamic_slice_in_dim(sums_by_row, rank * own_columns, own_columns, 1)
    projection_parts = [
        (start, order, exchange.done[f"projection{start}"]) for start, order in projection_orders
    ]
    zero = after(jnp.zeros((), f32), normed_terms)
    input_gradient = (
        grad_hidden + normalize_back(grad_normed, attention_gain, unit_one, inverse_one)
    ).astype(bf16)

    contract_gradient = jnp.broadcast_to(zero, contract_local.shape)
    for mask, block in exchange.done["contract"]:
        contract_gradient = put(
            contract_gradient, block, cut_place(mask, bits, contract_local.shape[0])
        )
    expand_gradient = jnp.broadcast_to(zero, expand_local.shape)
    for mask, block in exchange.done["expand"]:
        expand_gradient = put(
            expand_gradient, block, cut_place(mask, bits[::-1], expand_local.shape[0])
        )
    projection_gradient = jnp.broadcast_to(zero.astype(bf16), projection_local.shape)
    for start, order, blocks in projection_parts:
        for mask, block in blocks:
            projection_gradient = put(
                projection_gradient, block, start + cut_place(mask, order, cut)
            )
    projection_gradient = projection_gradient.reshape(features, 3, local_width).astype(f32)
    output_gradient = jnp.broadcast_to(zero, output_local.shape)
    for mask, block in exchange.done["output"]:
        output_gradient = put(
            output_gradient, block, cut_place(mask, bits, output_local.shape[0])
        )

    branch = branch_totals[0] + branch_arrived.astype(f32)
    layer_output = (local_live * (hidden + branch + contract_bias)).astype(bf16)
    query_value_gradient = sums_by_width[: 2 * local_width].reshape(2, local_width)
    expand_bias_gradient = sums_by_width[2 * local_width :]
    return (
        layer_output,
        input_gradient,
        sums_by_row[0],
        sums_by_row[1],
        projection_gradient,
        query_value_gradient,
        output_gradient,
        sums_by_row[2],
        sums_by_row[3],
        sums_by_row[4],
        expand_gradient,
        expand_bias_gradient,
        contract_gradient,
        sums_by_row[5],
    )


def solution(mesh):
    placed = (
        P(("dp", "tensor"), None),
        P(),
        P(),
        P(),
        P(None, None, "tensor"),
        P(None, "tensor"),
        P("tensor", None),
        P(),
        P(),
        P(),
        P(None, "tensor"),
        P("tensor"),
        P("tensor", None),
        P(),
        P(("dp", "tensor"), None),
    )
    return jax.shard_map(
        shards,
        mesh=mesh,
        in_specs=placed,
        out_specs=(
            P(("dp", "tensor"), None),
            P(("dp", "tensor"), None),
            P("tensor"),
            P("tensor"),
            P(None, None, "tensor"),
            P(None, "tensor"),
            P("tensor", None),
            P("tensor"),
            P("tensor"),
            P("tensor"),
            P(None, "tensor"),
            P("tensor"),
            P("tensor", None),
            P("tensor"),
        ),
        check_vma=False,
    )
```
